256 devices in a mesh: vocab: 16 (over z_lo, x, core), store: 16 (over z_hi, y).
Axes of the slice: x: 4, y: 4, z: 8 (z_hi: 4, z_lo: 2; z = z_hi * 2 + z_lo), core: 2. Of those that a mesh axis runs over, the one named last changes fastest.
Arguments:
- hidden_states: bfloat16 [512, 4096], P(('vocab', 'store')), may hold values from -100 to 100, as said below
- head: bfloat16 [128256, 4096], P(('vocab', 'store')), may hold values from -0.75 to 0.75
- proj_out: float32 [128256, 64], P(('vocab', 'store')), may hold values from -6 to 6
- proj_in: bfloat16 [4096, 64], replicated, may hold values from -0.09375 to 0.09375
- store: bfloat16 [2048, 4096], P('store'), may hold values from -0.25 to 0.25
- targets: int32 [512], replicated, may hold values from 0 to 128255
Outputs:
- scores: float32 [512, 2048], P('vocab', 'store')
The draws below stay inside these ranges and needn't reach their ends.
Inputs may be any that keep to these rules, and one draw needn't show every extreme that they name: `hidden_states`: real values; most entries of order one, some query rows a dozen times larger.
All inputs are finite; a program needn't handle non-finite values.
Results may differ from the reference program's by a relative error of at most 0.0015.
The reference program's roundings to bfloat16 on the way (of `kron`) count: a program that leaves them out, or rounds other values in their place, can miss the bound.
Values may be sent and summed in bfloat16 or wider, within the bound.
A program may use at most 320 MiB of HBM per device.

```python
import jax
import jax.numpy as jnp
from jax import lax

D = 4096
V = 128256
R = 64
Q = 512
NROWS = 2048


def draw_hidden_states(key, part):
    key = jax.random.fold_in(key, 11)
    first = jax.random.fold_in(key, 0)
    third = jax.random.fold_in(key, 2)
    base = jnp.clip(jax.random.normal(first, (Q, D), jnp.float32), -6.0, 6.0)
    strong = jax.random.randint(third, (Q, 1), 0, 16) == 0
    factor = jnp.where(strong, 12.0, 1.0)
    return (base * factor).astype(jnp.bfloat16)


def plant(values, key, low, largest):
    place = [jax.random.randint(jax.random.fold_in(key, axis), (), 0, length) for axis, length in enumerate(values.shape)]
    widest = values.shape.index(max(values.shape))
    beside = place[:widest] + [(place[widest] + 1) % values.shape[widest]] + place[widest + 1:]
    return values.at[tuple(place)].set(low).at[tuple(beside)].set(largest)


def steps_of(own_key, extent, cuts, low, high):
    loudness, own = 1.0, jax.random.fold_in(own_key, 6)
    for position, shards_of in cuts:
        heights = jnp.exp(jax.random.uniform(jax.random.fold_in(own, position), (shards_of,), jnp.float32, low / len(cuts), high / len(cuts)))
        loudness = loudness * jnp.repeat(heights, extent[position] // shards_of).reshape([-1 if axis == position else 1 for axis in range(len(extent))])
    return loudness


def gaussian(key, extent, scale, bound, cuts=(), dtype=jnp.bfloat16):
    entries = scale * jax.random.normal(key, extent, jnp.float32)
    if cuts:
        entries = entries * steps_of(key, extent, cuts, -0.22, 0.18)
    return jnp.clip(entries, -bound, bound).astype(dtype)


def setup_inputs(seed: int = 0) -> dict:
    key_of = jax.random.split(jax.random.key(seed), 7)
    return {
        "hidden_states": draw_hidden_states(jax.random.fold_in(key_of[6], 71), 0),
        "head": gaussian(key_of[1], (V, D), (3 * D ** -0.5), 0.75, ((0, 256),)),
        "proj_out": gaussian(key_of[2], (V, R), 1.0, 6.0, ((0, 256),), jnp.float32),
        "proj_in": gaussian(key_of[3], (D, R), D ** -0.5, 0.09375),
        "store": gaussian(key_of[4], (NROWS, R * R), 0.015625, 0.25, ((0, 16),)),
        "targets": plant(jax.random.randint(key_of[5], (Q,), 0, V), jax.random.fold_in(key_of[5], 1), 0, V - 1).astype(jnp.int32),
    }


def reference(hidden_states, head, proj_out, proj_in, store, targets):
    blocks = hidden_states.reshape(-1, 128, hidden_states.shape[1])
    target_blocks = targets.reshape(-1, 128)

    def vocab_block(pair):
        rows, wanted = pair
        logits = lax.dot_general(rows, head, (((1,), (1,)), ((), ())), preferred_element_type=jnp.float32)
        peak = jnp.max(logits, axis=1, keepdims=True)
        expd = jnp.exp(logits - peak)
        total = jnp.sum(expd, axis=1, keepdims=True)
        probs = expd / total
        summed = jnp.dot(probs, proj_out, precision=lax.Precision.HIGHEST, preferred_element_type=jnp.float32)
        return summed - jnp.take(proj_out, wanted, axis=0)

    vocab_side = lax.map(vocab_block, (blocks, target_blocks)).reshape(-1, proj_out.shape[1])
    width_side = jnp.dot(hidden_states, proj_in, preferred_element_type=jnp.float32)
    kron = (vocab_side[:, :, None] * width_side[:, None, :]).reshape(vocab_side.shape[0], -1).astype(jnp.bfloat16)
    return lax.dot_general(kron, store, (((1,), (1,)), ((), ())), preferred_element_type=jnp.float32)
```

```python
import functools

import jax
import jax.numpy as jnp
from jax import lax
from jax.experimental import pallas as pl
from jax.experimental.pallas import tpu as pltpu
from jax.sharding import PartitionSpec as P

MESH = pl.DeviceIdType.MESH
F32 = jnp.float32
BF16 = jnp.bfloat16
NT = (((1,), (1,)), ((), ()))


def kernel(
    hid, head, po, pin, store, tgt, out,
    zbuf, hbuf, head_v, po_v, w_v, pin_v, store_v, acc,
    tp, tb1, tb2, tb3, ts2, ts3, pm, rb1, rb2, rb3, rs2, rs3, wd, kron,
    lsem, csem_s, csem_r, zs, zr, gs, gr, ts, tr, rs, rr,
):
    nv, width = head.shape
    v = lax.axis_index("vocab")
    s = lax.axis_index("store")
    c = lax.rem(v, 2)
    x = lax.rem(lax.div(v, 2), 4)
    zl = lax.div(v, 8)
    zh = lax.div(s, 4)
    y = lax.rem(s, 4)
    z = zh * 2 + zl

    def dev(x_, y_, zl_, zh_, c_=None):
        c_ = c if c_ is None else c_
        return ((zl_ * 4 + x_) * 2 + c_, zh_ * 4 + y_)

    def plus(a, d, n):
        return lax.rem(a + (d + n), n)

    peer = dev(x, y, zl, zh, 1 - c)
    zpeers = []
    for d in range(1, 8):
        zz = plus(z, d, 8)
        zpeers.append(dev(x, y, lax.rem(zz, 2), lax.div(zz, 2)))
    xpeer = {d: dev(plus(x, d, 4), y, zl, zh) for d in (-1, 1)}
    ypeer = {d: dev(x, plus(y, d, 4), zl, zh) for d in (-1, 1)}
    offs = [(dx, dz) for dz in (0, 1) for dx in range(4)][1:]
    r1 = [(plus(x, dx, 4), lax.rem(zl + dz, 2)) for dx, dz in offs]
    r1dev = [dev(a, y, b, zh) for a, b in r1]
    r2dev = [dev(x, plus(y, d, 4), zl, zh) for d in (1, 2, 3)]
    r3dev = [dev(x, y, zl, plus(zh, d, 4)) for d in (1, 2, 3)]

    l_hid = pltpu.make_async_copy(hid, zbuf.at[zl * 4 + zh], lsem.at[0])
    l_po = pltpu.make_async_copy(po, po_v.at[0], lsem.at[1])
    l_head = pltpu.make_async_copy(head, head_v.at[0], lsem.at[2])
    l_pin = pltpu.make_async_copy(pin, pin_v, lsem.at[3])
    l_store = pltpu.make_async_copy(store, store_v, lsem.at[4])
    for l in (l_hid, l_po, l_head, l_pin, l_store):
        l.start()

    barrier = pltpu.get_barrier_semaphore()
    greet = zpeers + [dev(plus(x, d, 4), y, zl, zh) for d in (1, 2, 3)] + r2dev
    greet += [r1dev[k] for k, (dx, dz) in enumerate(offs) if dz and dx] + [peer]
    for other in greet:
        pl.semaphore_signal(barrier, inc=1, device_id=other, device_id_type=MESH)
    pl.semaphore_wait(barrier, len(greet))

    started = []

    def send(src, dst, ssem, rsem, to):
        copy = pltpu.make_async_remote_copy(
            src_ref=src, dst_ref=dst, send_sem=ssem, recv_sem=rsem,
            device_id=to, device_id_type=MESH,
        )
        copy.start()
        started.append(copy)
        return copy

    zcopies = [
        send(hid, zbuf.at[zl * 4 + zh], zs.at[k], zr.at[k], to)
        for k, to in enumerate(zpeers)
    ]
    c_po = send(po, po_v.at[1], csem_s.at[0], csem_r.at[0], peer)
    c_head = send(head, head_v.at[1], csem_s.at[1], csem_r.at[1], peer)

    def split(h):
        p = po_v[h]
        hi = p.astype(BF16).astype(F32)
        rest = p - hi
        mid = rest.astype(BF16).astype(F32)
        low = rest - mid
        w_v[h] = jnp.concatenate([hi, mid, low, jnp.zeros_like(p)], axis=1).astype(BF16)

    lane = lax.broadcasted_iota(jnp.int32, (1, 128), 1)
    first = lane < 64

    nq = 256
    row = lax.broadcasted_iota(jnp.int32, (nq, 1), 0)
    ry, rx, rzl, rzh, ri = (
        row // 64, (row // 16) % 4, (row // 8) % 2, (row // 2) % 4, row % 2,
    )
    query = 2 * (((rzl * 4 + rx) * 2 + c) * 16 + rzh * 4 + ry) + ri
    ids = lax.broadcasted_iota(jnp.int32, (1, 512), 1)
    wanted = jnp.sum(
        jnp.where(ids == query, tgt[...].astype(F32), 0.0), axis=1, keepdims=True
    )

    def sum_terms(a, b):
        half = a + pltpu.roll(a, 64, axis=1)
        return half + (b + pltpu.roll(b, 64, axis=1))

    def target_rows(h):
        base = (((v - c) + lax.rem(c + h, 2)) * 16 + s) * nv
        cols = (lax.broadcasted_iota(jnp.int32, (1, nv), 1) + base).astype(F32)
        hot = jnp.where(cols == wanted, 1.0, 0.0).astype(BF16)
        return jnp.dot(hot, w_v[h], preferred_element_type=F32)

    l_po.wait()
    split(0)
    t0 = target_rows(0)
    c_po.wait_recv()
    split(1)
    t01 = t0 + target_rows(1)
    t = sum_terms(t01[:, :128], t01[:, 128:]).reshape(4, 64, 128)
    tp[...] = jnp.where(first, t[:2], t[2:]).reshape(2, 4, 2, 8, 128)
    tcopies = [
        send(tp.at[:, a, b], tb1.at[k], ts.at[k], tr.at[k], r1dev[k])
        for k, (a, b) in enumerate(r1)
    ]

    l_hid.wait()
    for k in zcopies:
        k.wait_recv()
    place = y * 4 + x
    rows8 = lax.broadcasted_iota(jnp.int32, (8, 1), 0)
    for n in range(4):
        span = pl.ds(n * (width // 4), width // 4)
        halves = []
        for tile in range(2):
            made = jnp.zeros((8, width // 4), F32)
            for p in range(4):
                pair = zbuf[tile * 4 + p, :, span].astype(F32)
                for i in range(2):
                    made = jnp.where(rows8 == 2 * p + i, pair[i : i + 1], made)
            halves.append(made)
        hbuf[place, :, span] = jnp.concatenate(halves, axis=0).astype(BF16)

    half = width // 2
    quarter = width // 4

    class Order:
        def __init__(self, base, sem, apeer, bpeer, block):
            self.cols = pl.ds(base, half)
            self.part = {1: pl.ds(base, quarter), -1: pl.ds(base + quarter, quarter)}
            self.sem, self.apeer, self.bpeer, self.block = sem, apeer, bpeer, block
            self.near, self.far, self.bnear, self.bfar = {}, {}, {}, {}

        def put(self, j, block, cols, to):
            view = hbuf.at[block, :, cols]
            return send(view, view, gs.at[self.sem + j], gr.at[self.sem + j], to)

        def own(self):
            for k, d in enumerate((1, -1)):
                self.near[d] = self.put(k, self.block(0, 0), self.cols, self.apeer[d])

        def onward(self, j, da):
            for k, d in enumerate((1, -1)):
                self.bnear[da, d] = self.put(4 + j * 2 + k, self.block(da, 0), self.cols, self.bpeer[d])

        def pass_on(self, k, d):
            self.near[d].wait_recv()
            self.far[d] = self.put(2 + k, self.block(-d, 0), self.part[d], self.apeer[d])

        def bpass_on(self, j, da):
            for k, d in enumerate((1, -1)):
                self.bnear[da, d].wait_recv()
                self.bfar[da, d] = self.put(12 + j * 2 + k, self.block(da, -d), self.part[d], self.bpeer[d])

    orders = [
        Order(0, 0, xpeer, ypeer, lambda a, b: plus(y, b, 4) * 4 + plus(x, a, 4)),
        Order(half, 20, ypeer, xpeer, lambda a, b: plus(y, a, 4) * 4 + plus(x, b, 4)),
    ]
    for o in orders:
        o.own()
    for o in orders:
        o.onward(0, 0)
    for k, d in enumerate((1, -1)):
        for o in orders:
            o.pass_on(k, d)
            o.onward(1 + k, -d)

    total = tp[:, x, zl]
    for k, copy in enumerate(tcopies):
        copy.wait_recv()
        total = total + tb1[k]
    ts2[...] = total
    tcopies2 = [
        send(ts2, tb2.at[k], ts.at[7 + k], tr.at[7 + k], to) for k, to in enumerate(r2dev)
    ]

    for o in orders:
        o.bpass_on(0, 0)
    for o in orders:
        for d in (1, -1):
            o.far[d].wait_recv()
        o.onward(3, 2)
    for k, d in enumerate((1, -1)):
        for o in orders:
            o.bpass_on(1 + k, -d)

    for k, copy in enumerate(tcopies2):
        copy.wait_recv()
        total = total + tb2[k]
    ts3[...] = total
    tcopies3 = [
        send(ts3, tb3.at[k], ts.at[10 + k], tr.at[10 + k], to) for k, to in enumerate(r3dev)
    ]

    for o in orders:
        o.bpass_on(3, 2)
    for k, copy in enumerate(tcopies3):
        copy.wait_recv()
        total = total + tb3[k]
    trows = total

    l_head.wait()
    c_head.wait_recv()
    for o in orders:
        for copy in o.bfar.values():
            copy.wait_recv()

    step = 512
    acc[...] = jnp.zeros_like(acc)

    def logits(i, carry):
        span = pl.ds(pl.multiple_of(i * step, step), step)
        left = hbuf[:, :, span].reshape(nq, step)
        for h in range(2):
            acc[h] += lax.dot_general(left, head_v[h, :, span], NT, preferred_element_type=F32)
        return carry

    lax.fori_loop(0, width // step, logits, 0)

    peak = jnp.maximum(
        jnp.max(acc[0], axis=1, keepdims=True), jnp.max(acc[1], axis=1, keepdims=True)
    )
    sides = []
    denom = jnp.zeros((nq, 1), F32)
    for h in range(2):
        e = jnp.exp(acc[h] - peak)
        denom = denom + jnp.sum(e, axis=1, keepdims=True)
        hi = e.astype(BF16)
        low = (e - hi.astype(F32)).astype(BF16)
        sides.append(
            jnp.dot(hi, w_v[h], preferred_element_type=F32)
            + jnp.dot(low, w_v[h], preferred_element_type=F32)
        )
    both = sides[0] + sides[1]
    both = sum_terms(both[:, :128], both[:, 128:])
    is_peak = (lane >= 64) & (lane < 96)
    packed = jnp.where(first, both, jnp.where(is_peak, peak, denom))
    pm[...] = packed.reshape(4, 4, 2, 8, 128)
    rcopies = [
        send(pm.at[:, a, b], rb1.at[k], rs.at[k], rr.at[k], r1dev[k])
        for k, (a, b) in enumerate(r1)
    ]

    l_pin.wait()

    def widths(i, carry):
        span = pl.ds(pl.multiple_of(i * step, step), step)
        left = jnp.concatenate([hbuf[b * 4 + x, :, span] for b in range(4)], axis=0)
        return carry + jnp.dot(left, pin_v[span, :], preferred_element_type=F32)

    w = lax.fori_loop(0, width // step, widths, jnp.zeros((64, 64), F32))
    wd[...] = jnp.concatenate([w, w], axis=1).reshape(4, 2, 8, 128)
    width2 = wd[:, zl].reshape(32, 128)

    def combine(parts):
        most = parts[0]
        for p in parts[1:]:
            most = jnp.maximum(most, p)
        m = most[:, 64:65]
        out_ = None
        for p in parts:
            term = p * jnp.exp(p[:, 64:65] - m)
            out_ = term if out_ is None else out_ + term
        return jnp.where(is_peak, most, out_)

    def waited(copies, buf):
        got = []
        for k, copy in enumerate(copies):
            copy.wait_recv()
            got.append(buf[k].reshape(32, 128))
        return got

    mine = pm[:, x, zl].reshape(32, 128)
    mine = combine([mine] + waited(rcopies, rb1))
    rs2[...] = mine.reshape(4, 8, 128)
    rcopies = [send(rs2, rb2.at[k], rs.at[7 + k], rr.at[7 + k], to) for k, to in enumerate(r2dev)]
    mine = combine([mine] + waited(rcopies, rb2))
    rs3[...] = mine.reshape(4, 8, 128)
    rcopies = [send(rs3, rb3.at[k], rs.at[10 + k], rr.at[10 + k], to) for k, to in enumerate(r3dev)]
    mine = combine([mine] + waited(rcopies, rb3))

    tflat = trows.reshape(16, 128)
    side = mine / mine[:, 96:97] - jnp.concatenate([tflat, pltpu.roll(tflat, 64, axis=1)], axis=0)
    for b in range(32):
        pair = jnp.where(first, side[:, 2 * b : 2 * b + 1], side[:, 2 * b + 1 : 2 * b + 2])
        kron[:, b * 128 : (b + 1) * 128] = (pair * width2).astype(BF16)
    l_store.wait()
    scores = lax.dot_general(kron[...], store_v[...], NT, preferred_element_type=F32)
    out[...] = scores.reshape(4, 8, 128)

    for copy in started:
        copy.wait_send()


def local(hidden_states, head, proj_out, proj_in, store, targets):
    nv, width = head.shape
    vm = pltpu.VMEM
    dma = pltpu.SemaphoreType.DMA
    got = pl.pallas_call(
        kernel,
        out_shape=jax.ShapeDtypeStruct((4, 8, 128), F32),
        in_specs=[pl.BlockSpec(memory_space=pl.ANY)] * 5 + [pl.BlockSpec(memory_space=pltpu.VMEM)],
        out_specs=pl.BlockSpec(memory_space=pltpu.VMEM),
        scratch_shapes=[
            vm((8, 2, width), BF16),
            vm((16, 16, width), BF16),
            vm((2, nv, width), BF16),
            vm((2, nv, 64), F32),
            vm((2, nv, 256), BF16),
            vm((width, 64), BF16),
            vm((128, width), BF16),
            vm((2, 256, nv), F32),
            vm((2, 4, 2, 8, 128), F32),
            vm((7, 2, 8, 128), F32),
            vm((3, 2, 8, 128), F32),
            vm((3, 2, 8, 128), F32),
            vm((2, 8, 128), F32),
            vm((2, 8, 128), F32),
            vm((4, 4, 2, 8, 128), F32),
            vm((7, 4, 8, 128), F32),
            vm((3, 4, 8, 128), F32),
            vm((3, 4, 8, 128), F32),
            vm((4, 8, 128), F32),
            vm((4, 8, 128), F32),
            vm((4, 2, 8, 128), F32),
            vm((32, width), BF16),
            dma((5,)), dma((2,)), dma((2,)), dma((7,)), dma((7,)),
            dma((40,)), dma((40,)), dma((13,)), dma((13,)), dma((13,)), dma((13,)),
        ],
        compiler_params=pltpu.CompilerParams(
            collective_id=0, has_side_effects=True, vmem_limit_bytes=40 * 2**20
        ),
        cost_estimate=pl.CostEstimate(flops=2 * 10**9, bytes_accessed=10**7, transcendentals=0),
    )(hidden_states, head, proj_out, proj_in, store, targets.reshape(1, -1))
    return got.reshape(4, 4, 2, 128).transpose(1, 0, 2, 3).reshape(32, 128)


def solution(mesh):
    placed = (
        P(("vocab", "store"), None),
        P(("vocab", "store"), None),
        P(("vocab", "store"), None),
        P(),
        P("store", None),
        P(),
    )
    return jax.shard_map(
        local, mesh=mesh, in_specs=placed, out_specs=P("vocab", "store"), check_vma=False
    )
```

```python
import functools

import jax
import jax.numpy as jnp
from jax import lax
from jax.experimental import pallas as pl
from jax.experimental.pallas import tpu as pltpu
from jax.sharding import PartitionSpec as P

MESH = pl.DeviceIdType.MESH
ZSHARE = 512
F32 = jnp.float32
BF16 = jnp.bfloat16
NT = (((1,), (1,)), ((), ()))


def kernel(
    hid, head, po, pin, store, tgt, out,
    tgt_v, zbuf, hbuf, head_v, po_v, w_v, pin_v, store_v, acc,
    tp, tb1, tb2, tb3, ts2, ts3, pm, rb1, rb2, rb3, rs2, rs3, wd, kron,
    lsem, csem_s, csem_r, zs, zr, gs, gr, ts, tr, rs, rr, dbuf, ds, dr,
):
    nv, width = head.shape
    v = lax.axis_index("vocab")
    s = lax.axis_index("store")
    c = lax.rem(v, 2)
    x = lax.rem(lax.div(v, 2), 4)
    zl = lax.div(v, 8)
    zh = lax.div(s, 4)
    y = lax.rem(s, 4)
    z = zh * 2 + zl

    def dev(x_, y_, zl_, zh_, c_=None):
        c_ = c if c_ is None else c_
        return ((zl_ * 4 + x_) * 2 + c_, zh_ * 4 + y_)

    def plus(a, d, n):
        return lax.rem(a + (d + n), n)

    peer = dev(x, y, zl, zh, 1 - c)
    zpeers = []
    for d in range(1, 8):
        zz = plus(z, d, 8)
        zpeers.append(dev(x, y, lax.rem(zz, 2), lax.div(zz, 2)))
    xpeer = {d: dev(plus(x, d, 4), y, zl, zh) for d in (-1, 1, 2)}
    ypeer = {d: dev(x, plus(y, d, 4), zl, zh) for d in (-1, 1, 2)}
    offs = [(dx, dz) for dz in (0, 1) for dx in range(4)][1:]
    r1 = [(plus(x, dx, 4), lax.rem(zl + dz, 2)) for dx, dz in offs]
    r1dev = [dev(a, y, b, zh) for a, b in r1]
    r2dev = [dev(x, plus(y, d, 4), zl, zh) for d in (1, 2, 3)]
    r3dev = [dev(x, y, zl, plus(zh, d, 4)) for d in (1, 2, 3)]

    l_hid = pltpu.make_async_copy(hid, zbuf.at[zl * 4 + zh], lsem.at[0])
    l_last = pltpu.make_async_copy(
        hid.at[:, pl.ds(width - ZSHARE, ZSHARE)], dbuf.at[y, x, zl * 4 + zh], lsem.at[6]
    )
    l_po = pltpu.make_async_copy(po, po_v.at[0], lsem.at[1])
    l_head = pltpu.make_async_copy(head, head_v.at[0], lsem.at[2])
    l_pin = pltpu.make_async_copy(pin, pin_v, lsem.at[3])
    l_store = pltpu.make_async_copy(store, store_v, lsem.at[4])
    l_tgt = pltpu.make_async_copy(tgt, tgt_v, lsem.at[5])
    for l in (l_hid, l_last, l_po, l_tgt, l_head, l_pin, l_store):
        l.start()

    barrier = pltpu.get_barrier_semaphore()
    greet = zpeers + [dev(plus(x, d, 4), y, zl, zh) for d in (1, 2, 3)] + r2dev
    greet += [r1dev[k] for k, (dx, dz) in enumerate(offs) if dz and dx] + [peer]
    for other in greet:
        pl.semaphore_signal(barrier, inc=1, device_id=other, device_id_type=MESH)
    pl.semaphore_wait(barrier, len(greet))

    zcols = ZSHARE
    half = (width - zcols) // 2
    xycols, dcols = pl.ds(0, 2 * half), pl.ds(2 * half, zcols)

    started = []

    def send(src, dst, ssem, rsem, to):
        copy = pltpu.make_async_remote_copy(
            src_ref=src, dst_ref=dst, send_sem=ssem, recv_sem=rsem,
            device_id=to, device_id_type=MESH,
        )
        copy.start()
        started.append(copy)
        return copy

    here = zl * 4 + zh
    zcopies = [
        send(hid.at[:, xycols], zbuf.at[here, :, xycols], zs.at[k], zr.at[k], to)
        for k, to in enumerate(zpeers)
    ]
    xall = [xpeer[d] for d in (1, -1, 2)]
    yall = [ypeer[d] for d in (1, -1, 2)]
    dxs = [
        send(hid.at[:, dcols], dbuf.at[y, x, here], ds.at[k], dr.at[k], to)
        for k, to in enumerate(xall)
    ]
    c_po = send(po, po_v.at[1], csem_s.at[0], csem_r.at[0], peer)
    c_head = send(head, head_v.at[1], csem_s.at[1], csem_r.at[1], peer)

    def split(h):
        p = po_v[h]
        hi = p.astype(BF16).astype(F32)
        rest = p - hi
        mid = rest.astype(BF16).astype(F32)
        low = rest - mid
        w_v[h] = jnp.concatenate([hi, mid, low, jnp.zeros_like(p)], axis=0).astype(BF16)

    lane = lax.broadcasted_iota(jnp.int32, (1, 128), 1)
    first = lane < 64

    nq = 256
    row = lax.broadcasted_iota(jnp.int32, (nq, 1), 0)
    ry, rx, rzl, rzh, ri = (
        row // 64, (row // 16) % 4, (row // 8) % 2, (row // 2) % 4, row % 2,
    )
    query = 2 * (((rzl * 4 + rx) * 2 + c) * 16 + rzh * 4 + ry) + ri
    ids = lax.broadcasted_iota(jnp.int32, (1, 512), 1)
    l_tgt.wait()
    wanted = jnp.sum(
        jnp.where(ids == query, tgt_v[...].astype(F32), 0.0), axis=1, keepdims=True
    )

    def sum_terms(a, b):
        half = a + pltpu.roll(a, 64, axis=1)
        return half + (b + pltpu.roll(b, 64, axis=1))

    def target_rows(h):
        base = (((v - c) + lax.rem(c + h, 2)) * 16 + s) * nv
        cols = (lax.broadcasted_iota(jnp.int32, (1, nv), 1) + base).astype(F32)
        hot = jnp.where(cols == wanted, 1.0, 0.0).astype(BF16)
        return lax.dot_general(hot, w_v[h], NT, preferred_element_type=F32)

    l_po.wait()
    split(0)
    t0 = target_rows(0)
    c_po.wait_recv()
    split(1)
    t01 = t0 + target_rows(1)
    t = sum_terms(t01[:, :128], t01[:, 128:]).reshape(4, 64, 128)
    tp[...] = jnp.where(first, t[:2], t[2:]).reshape(2, 4, 2, 8, 128)
    tcopies = [
        send(tp.at[:, a, b], tb1.at[k], ts.at[k], tr.at[k], r1dev[k])
        for k, (a, b) in enumerate(r1)
    ]

    l_last.wait()
    for copy in dxs:
        copy.wait_recv()
    dcolumn = dbuf.at[y, :, here]
    dys = [send(dcolumn, dcolumn, ds.at[3 + k], dr.at[3 + k], to) for k, to in enumerate(yall)]
    l_hid.wait()
    for k in zcopies:
        k.wait_recv()
    rows8 = lax.broadcasted_iota(jnp.int32, (8, 1), 0)

    def sixteen(piece):
        halves = []
        for tile in range(2):
            made = None
            for p in range(4):
                pair = piece(tile * 4 + p).astype(F32)
                for i in range(2):
                    row_ = jnp.broadcast_to(pair[i : i + 1], (8, pair.shape[1]))
                    made = row_ if made is None else jnp.where(rows8 == 2 * p + i, row_, made)
            halves.append(made)
        return jnp.concatenate(halves, axis=0).astype(BF16)

    for n in range(0, 2 * half, 512):
        span = pl.ds(n, min(512, 2 * half - n))
        hbuf[y, x, :, span] = sixteen(lambda p: zbuf[p, :, span])

    quarter = (half // 256) * 128

    class Order:
        def __init__(self, base, sem, apeer, bpeer, block):
            self.cols = pl.ds(base, half)
            self.part = {1: pl.ds(base, quarter), -1: pl.ds(base + quarter, half - quarter)}
            self.sem, self.apeer, self.bpeer, self.block = sem, apeer, bpeer, block
            self.near, self.bnear, self.bfar = {}, {}, {}

        def put(self, j, block, cols, to):
            view = hbuf.at[block[0], block[1], :, cols]
            return send(view, view, gs.at[self.sem + j], gr.at[self.sem + j], to)

        def own(self):
            for k, d in enumerate((1, -1, 2)):
                self.near[d] = self.put(k, self.block(0, 0), self.cols, self.apeer[d])

        def onward(self, j, da):
            for k, d in enumerate((1, -1)):
                self.bnear[da, d] = self.put(4 + j * 2 + k, self.block(da, 0), self.cols, self.bpeer[d])
            if j in (3,):
                self.bfar[da, 2] = self.put(12 + j * 2, self.block(da, 0), self.cols, self.bpeer[2])

        def bpass_on(self, j, da):
            for k, d in enumerate((1, -1)):
                self.bnear[da, d].wait_recv()
                if j in (3,):
                    continue
                self.bfar[da, d] = self.put(12 + j * 2 + k, self.block(da, -d), self.part[d], self.bpeer[d])

    orders = [
        Order(0, 0, xpeer, ypeer, lambda a, b: (plus(y, b, 4), plus(x, a, 4))),
        Order(half, 20, ypeer, xpeer, lambda a, b: (plus(y, a, 4), plus(x, b, 4))),
    ]
    for o in orders:
        o.own()
    for o in orders:
        o.onward(0, 0)
    acc[...] = jnp.zeros_like(acc)
    for copy in dys:
        copy.wait_recv()
    dplane = dbuf.at[:, :, here]
    dzs = [
        send(dplane, dplane, ds.at[6 + k], dr.at[6 + k], to) for k, to in enumerate(zpeers)
    ]
    for k, d in enumerate((1, -1)):
        for o in orders:
            o.near[d].wait_recv()
            o.onward(1 + k, -d)

    total = tp[:, x, zl]
    for k, copy in enumerate(tcopies):
        copy.wait_recv()
        total = total + tb1[k]
    ts2[...] = total
    tcopies2 = [
        send(ts2, tb2.at[k], ts.at[7 + k], tr.at[7 + k], to) for k, to in enumerate(r2dev)
    ]

    for o in orders:
        o.bpass_on(0, 0)
    for o in orders:
        o.near[2].wait_recv()
        o.onward(3, 2)
    for k, d in enumerate((1, -1)):
        for o in orders:
            o.bpass_on(1 + k, -d)

    l_head.wait()
    c_head.wait_recv()

    for k, copy in enumerate(tcopies2):
        copy.wait_recv()
        total = total + tb2[k]
    ts3[...] = total
    tcopies3 = [
        send(ts3, tb3.at[k], ts.at[10 + k], tr.at[10 + k], to) for k, to in enumerate(r3dev)
    ]

    for o in orders:
        o.bpass_on(3, 2)
    for k, copy in enumerate(tcopies3):
        copy.wait_recv()
        total = total + tb3[k]
    trows = total

    for copy in dzs:
        copy.wait_recv()

    def last_columns(k, carry):
        b, a = lax.div(k, 4), lax.rem(k, 4)
        hbuf[b, a, :, dcols] = sixteen(lambda p: dbuf[b, a, p])
        return carry

    lax.fori_loop(0, 16, last_columns, 0)
    for o in orders:
        for copy in o.bfar.values():
            copy.wait_recv()
    for k in range(0, width, 4096):
        span = pl.ds(k, 4096)
        left = hbuf[:, :, :, span].reshape(nq, 4096)
        for h in range(2):
            part = lax.dot_general(left, head_v[h, :, span], NT, preferred_element_type=F32)
            acc[h] = part.reshape(4, 4, 16, nv) + (acc[h] if k else 0.0)

    step = 512
    flat = [acc[h].reshape(nq, nv) for h in range(2)]
    peak = jnp.maximum(
        jnp.max(flat[0], axis=1, keepdims=True), jnp.max(flat[1], axis=1, keepdims=True)
    )
    sides = []
    denom = jnp.zeros((nq, 1), F32)
    for h in range(2):
        e = jnp.exp(flat[h] - peak)
        denom = denom + jnp.sum(e, axis=1, keepdims=True)
        hi = e.astype(BF16)
        low = (e - hi.astype(F32)).astype(BF16)
        sides.append(
            lax.dot_general(hi, w_v[h], NT, preferred_element_type=F32)
            + lax.dot_general(low, w_v[h], NT, preferred_element_type=F32)
        )
    both = sides[0] + sides[1]
    both = sum_terms(both[:, :128], both[:, 128:])
    is_peak = (lane >= 64) & (lane < 96)
    packed = jnp.where(first, both, jnp.where(is_peak, peak, denom))
    pm[...] = packed.reshape(4, 4, 2, 8, 128)
    rcopies = [
        send(pm.at[:, a, b], rb1.at[k], rs.at[k], rr.at[k], r1dev[k])
        for k, (a, b) in enumerate(r1)
    ]

    l_pin.wait()

    def widths(i, carry):
        span = pl.ds(pl.multiple_of(i * step, step), step)
        left = hbuf[:, x, :, span].reshape(64, step)
        return carry + lax.dot_general(left, pin_v[:, span], NT, preferred_element_type=F32)

    w = lax.fori_loop(0, width // step, widths, jnp.zeros((64, 64), F32))
    wd[...] = jnp.concatenate([w, w], axis=1).reshape(4, 2, 8, 128)
    width2 = wd[:, zl].reshape(32, 128)

    def combine(parts):
        most = parts[0]
        for p in parts[1:]:
            most = jnp.maximum(most, p)
        m = most[:, 64:65]
        out_ = None
        for p in parts:
            term = p * jnp.exp(p[:, 64:65] - m)
            out_ = term if out_ is None else out_ + term
        return jnp.where(is_peak, most, out_)

    def waited(copies, buf):
        got = []
        for k, copy in enumerate(copies):
            copy.wait_recv()
            got.append(buf[k].reshape(32, 128))
        return got

    mine = pm[:, x, zl].reshape(32, 128)
    mine = combine([mine] + waited(rcopies, rb1))
    rs2[...] = mine.reshape(4, 8, 128)
    rcopies = [send(rs2, rb2.at[k], rs.at[7 + k], rr.at[7 + k], to) for k, to in enumerate(r2dev)]
    mine = combine([mine] + waited(rcopies, rb2))
    rs3[...] = mine.reshape(4, 8, 128)
    rcopies = [send(rs3, rb3.at[k], rs.at[10 + k], rr.at[10 + k], to) for k, to in enumerate(r3dev)]
    mine = combine([mine] + waited(rcopies, rb3))

    tflat = trows.reshape(16, 128)
    side = mine / mine[:, 96:97] - jnp.concatenate([tflat, pltpu.roll(tflat, 64, axis=1)], axis=0)
    for b in range(32):
        pair = jnp.where(first, side[:, 2 * b : 2 * b + 1], side[:, 2 * b + 1 : 2 * b + 2])
        kron[:, b * 128 : (b + 1) * 128] = (pair * width2).astype(BF16)
    l_store.wait()
    scores = lax.dot_general(kron[...], store_v[...], NT, preferred_element_type=F32)
    out[...] = scores.reshape(4, 8, 128)

    for copy in started:
        copy.wait_send()


def local(hidden_states, head, proj_out, proj_in, store, targets):
    nv, width = head.shape
    vm = pltpu.VMEM
    dma = pltpu.SemaphoreType.DMA
    got = pl.pallas_call(
        kernel,
        out_shape=jax.ShapeDtypeStruct((4, 8, 128), F32),
        in_specs=[pl.BlockSpec(memory_space=pltpu.HBM)] * 6,
        out_specs=pl.BlockSpec(memory_space=pltpu.VMEM),
        scratch_shapes=[
            vm((1, 512), jnp.int32),
            vm((8, 2, width), BF16),
            vm((4, 4, 16, width), BF16),
            vm((2, nv, width), BF16),
            vm((2, 64, nv), F32),
            vm((2, 256, nv), BF16),
            vm((64, width), BF16),
            vm((128, width), BF16),
            vm((2, 4, 4, 16, nv), F32),
            vm((2, 4, 2, 8, 128), F32),
            vm((7, 2, 8, 128), F32),
            vm((3, 2, 8, 128), F32),
            vm((3, 2, 8, 128), F32),
            vm((2, 8, 128), F32),
            vm((2, 8, 128), F32),
            vm((4, 4, 2, 8, 128), F32),
            vm((7, 4, 8, 128), F32),
            vm((3, 4, 8, 128), F32),
            vm((3, 4, 8, 128), F32),
            vm((4, 8, 128), F32),
            vm((4, 8, 128), F32),
            vm((4, 2, 8, 128), F32),
            vm((32, width), BF16),
            dma((7,)), dma((2,)), dma((2,)), dma((7,)), dma((7,)),
            dma((40,)), dma((40,)), dma((13,)), dma((13,)), dma((13,)), dma((13,)),
            vm((4, 4, 8, 2, ZSHARE), BF16), dma((13,)), dma((13,)),
        ],
        compiler_params=pltpu.CompilerParams(
            collective_id=0, has_side_effects=True, vmem_limit_bytes=64 * 2**20 - 2**16
        ),
        cost_estimate=pl.CostEstimate(flops=2 * 10**9, bytes_accessed=10**7, transcendentals=0),
    )(hidden_states, head, proj_out.T, proj_in.T, store, targets.reshape(1, -1))
    return got.reshape(4, 4, 2, 128).transpose(1, 0, 2, 3).reshape(32, 128)


def solution(mesh):
    placed = (
        P(("vocab", "store"), None),
        P(("vocab", "store"), None),
        P(("vocab", "store"), None),
        P(),
        P("store", None),
        P(),
    )
    return jax.shard_map(
        local, mesh=mesh, in_specs=placed, out_specs=P("vocab", "store"), check_vma=False
    )
```

```python
import functools

import jax
import jax.numpy as jnp
from jax import lax
from jax.experimental import pallas as pl
from jax.experimental.pallas import tpu as pltpu
from jax.sharding import PartitionSpec as P

MESH = pl.DeviceIdType.MESH
ZSHARE = 768
F32 = jnp.float32
BF16 = jnp.bfloat16
NT = (((1,), (1,)), ((), ()))


def kernel(
    hid, head, po, pin, store, tgt, out,
    tgt_v, zbuf, hbuf, head_v, po_v, w_v, pin_v, store_v, acc,
    pm, rb1, rb2, rb3, rs2, rs3, wd, kron,
    lsem, csem_s, csem_r, zs, zr, gs, gr, rs, rr, dbuf, ds, dr,
):
    nv, width = head.shape
    v = lax.axis_index("vocab")
    s = lax.axis_index("store")
    c = lax.rem(v, 2)
    x = lax.rem(lax.div(v, 2), 4)
    zl = lax.div(v, 8)
    zh = lax.div(s, 4)
    y = lax.rem(s, 4)
    z = zh * 2 + zl

    def dev(x_, y_, zl_, zh_, c_=None):
        c_ = c if c_ is None else c_
        return ((zl_ * 4 + x_) * 2 + c_, zh_ * 4 + y_)

    def plus(a, d, n):
        return lax.rem(a + (d + n), n)

    peer = dev(x, y, zl, zh, 1 - c)
    zpeers = []
    for d in (4, 3, 5, 2, 6, 1, 7):
        zz = plus(z, d, 8)
        zpeers.append(dev(x, y, lax.rem(zz, 2), lax.div(zz, 2)))
    xpeer = {d: dev(plus(x, d, 4), y, zl, zh) for d in (-1, 1, 2)}
    ypeer = {d: dev(x, plus(y, d, 4), zl, zh) for d in (-1, 1, 2)}
    offs = [(2, 1), (1, 1), (3, 1), (2, 0), (1, 0), (3, 0), (0, 1)]
    r1 = [(plus(x, dx, 4), lax.rem(zl + dz, 2)) for dx, dz in offs]
    r1dev = [dev(a, y, b, zh) for a, b in r1]
    r2dev = [dev(x, plus(y, d, 4), zl, zh) for d in (2, 1, 3)]
    r3dev = [dev(x, y, zl, plus(zh, d, 4)) for d in (2, 1, 3)]

    l_hid = pltpu.make_async_copy(hid, zbuf.at[zl * 4 + zh], lsem.at[0])
    l_last = pltpu.make_async_copy(
        hid.at[:, pl.ds(width - ZSHARE, ZSHARE)], dbuf.at[y, x, zl * 4 + zh], lsem.at[6]
    )
    l_po = pltpu.make_async_copy(po, po_v.at[0], lsem.at[1])
    l_head = pltpu.make_async_copy(head, head_v.at[0], lsem.at[2])
    l_pin = pltpu.make_async_copy(pin, pin_v, lsem.at[3])
    l_store = pltpu.make_async_copy(store, store_v, lsem.at[4])
    l_tgt = pltpu.make_async_copy(tgt, tgt_v, lsem.at[5])
    for l in (l_hid, l_last, l_po, l_tgt, l_head, l_pin, l_store):
        l.start()

    barrier = pltpu.get_barrier_semaphore()
    greet = zpeers + [dev(plus(x, d, 4), y, zl, zh) for d in (1, 2, 3)] + r2dev
    greet += [r1dev[k] for k, (dx, dz) in enumerate(offs) if dz and dx] + [peer]
    for other in greet:
        pl.semaphore_signal(barrier, inc=1, device_id=other, device_id_type=MESH)
    pl.semaphore_wait(barrier, len(greet))

    zcols = ZSHARE
    half = (width - zcols) // 2
    xycols, dcols = pl.ds(0, 2 * half), pl.ds(2 * half, zcols)

    started = []

    def send(src, dst, ssem, rsem, to):
        copy = pltpu.make_async_remote_copy(
            src_ref=src, dst_ref=dst, send_sem=ssem, recv_sem=rsem,
            device_id=to, device_id_type=MESH,
        )
        copy.start()
        started.append(copy)
        return copy

    here = zl * 4 + zh
    l_hid.wait()
    l_last.wait()
    zcopies = [
        send(zbuf.at[here, :, xycols], zbuf.at[here, :, xycols], zs.at[k], zr.at[k], to)
        for k, to in enumerate(zpeers)
    ]
    xall = [xpeer[d] for d in (2, 1, -1)]
    yall = [ypeer[d] for d in (2, 1, -1)]
    dxs = [
        send(dbuf.at[y, x, here], dbuf.at[y, x, here], ds.at[k], dr.at[k], to)
        for k, to in enumerate(xall)
    ]
    c_po = send(po, po_v.at[1], csem_s.at[0], csem_r.at[0], peer)
    c_head = send(head, head_v.at[1], csem_s.at[1], csem_r.at[1], peer)

    def split(h):
        p = po_v[h]
        hi = p.astype(BF16).astype(F32)
        rest = p - hi
        mid = rest.astype(BF16).astype(F32)
        low = rest - mid
        w_v[h] = jnp.concatenate([hi, mid, low, jnp.zeros_like(p)], axis=0).astype(BF16)

    lane = lax.broadcasted_iota(jnp.int32, (1, 128), 1)
    first = lane < 64

    nq = 256
    row = lax.broadcasted_iota(jnp.int32, (nq, 1), 0)
    ry, rx, rzl, rzh, ri = (
        row // 64, (row // 16) % 4, (row // 8) % 2, (row // 2) % 4, row % 2,
    )
    query = 2 * (((rzl * 4 + rx) * 2 + c) * 16 + rzh * 4 + ry) + ri
    ids = lax.broadcasted_iota(jnp.int32, (1, 512), 1)
    l_tgt.wait()
    wanted = jnp.sum(
        jnp.where(ids == query, tgt_v[...].astype(F32), 0.0), axis=1, keepdims=True
    )

    def sum_terms(a, b):
        half = a + pltpu.roll(a, 64, axis=1)
        return half + (b + pltpu.roll(b, 64, axis=1))

    def target_rows(h):
        base = (((v - c) + lax.rem(c + h, 2)) * 16 + s) * nv
        cols = (lax.broadcasted_iota(jnp.int32, (1, nv), 1) + base).astype(F32)
        hot = jnp.where(cols == wanted, 1.0, 0.0).astype(BF16)
        return lax.dot_general(hot, w_v[h], NT, preferred_element_type=F32)

    l_po.wait()
    split(0)
    t0 = target_rows(0)
    c_po.wait_recv()
    split(1)
    t01 = t0 + target_rows(1)
    t = sum_terms(t01[:, :128], t01[:, 128:]).reshape(4, 64, 128)
    pm[4:] = jnp.where(first, t[:2], t[2:]).reshape(2, 4, 2, 8, 128)
    for copy in dxs:
        copy.wait_recv()
    dcolumn = dbuf.at[y, :, here]
    dys = [send(dcolumn, dcolumn, ds.at[3 + k], dr.at[3 + k], to) for k, to in enumerate(yall)]
    for k in zcopies:
        k.wait_recv()
    rows8 = lax.broadcasted_iota(jnp.int32, (8, 1), 0)

    def sixteen(piece):
        halves = []
        for tile in range(2):
            made = None
            for p in range(4):
                pair = piece(tile * 4 + p).astype(F32)
                for i in range(2):
                    row_ = jnp.broadcast_to(pair[i : i + 1], (8, pair.shape[1]))
                    made = row_ if made is None else jnp.where(rows8 == 2 * p + i, row_, made)
            halves.append(made)
        return jnp.concatenate(halves, axis=0).astype(BF16)

    for n in range(0, 2 * half, 512):
        span = pl.ds(n, min(512, 2 * half - n))
        hbuf[y, x, :, span] = sixteen(lambda p: zbuf[p, :, span])

    quarter = (half // 256) * 128

    class Order:
        def __init__(self, base, sem, apeer, bpeer, block):
            self.cols = pl.ds(base, half)
            self.part = {1: pl.ds(base, quarter), -1: pl.ds(base + quarter, half - quarter)}
            self.sem, self.apeer, self.bpeer, self.block = sem, apeer, bpeer, block
            self.near, self.bnear, self.bfar = {}, {}, {}

        def put(self, j, block, cols, to):
            view = hbuf.at[block[0], block[1], :, cols]
            return send(view, view, gs.at[self.sem + j], gr.at[self.sem + j], to)

        def own(self):
            for k, d in enumerate((1, -1, 2)):
                self.near[d] = self.put(k, self.block(0, 0), self.cols, self.apeer[d])

        def onward(self, j, da):
            for k, d in enumerate((1, -1)):
                self.bnear[da, d] = self.put(4 + j * 2 + k, self.block(da, 0), self.cols, self.bpeer[d])
            if j in (2, 3,):
                self.bfar[da, 2] = self.put(12 + j * 2, self.block(da, 0), self.cols, self.bpeer[2])

        def bpass_on(self, j, da):
            for k, d in enumerate((1, -1)):
                self.bnear[da, d].wait_recv()
                if j in (2, 3,):
                    continue
                self.bfar[da, d] = self.put(12 + j * 2 + k, self.block(da, -d), self.part[d], self.bpeer[d])

    orders = [
        Order(0, 0, xpeer, ypeer, lambda a, b: (plus(y, b, 4), plus(x, a, 4))),
        Order(half, 20, ypeer, xpeer, lambda a, b: (plus(y, a, 4), plus(x, b, 4))),
    ]
    for o in orders:
        o.own()
    for o in orders:
        o.onward(0, 0)
    for copy in dys:
        copy.wait_recv()
    dplane = dbuf.at[:, :, here]
    dzs = [
        send(dplane, dplane, ds.at[6 + k], dr.at[6 + k], to) for k, to in enumerate(zpeers)
    ]
    for k, d in enumerate((1, -1)):
        for o in orders:
            o.near[d].wait_recv()
            o.onward(1 + k, -d)

    for o in orders:
        o.bpass_on(0, 0)
    for o in orders:
        o.near[2].wait_recv()
        o.onward(3, 2)
    for k, d in enumerate((1, -1)):
        for o in orders:
            o.bpass_on(1 + k, -d)

    l_head.wait()
    c_head.wait_recv()

    for o in orders:
        o.bpass_on(3, 2)
    for copy in dzs:
        copy.wait_recv()

    def last_columns(k, carry):
        b, a = lax.div(k, 4), lax.rem(k, 4)
        hbuf[b, a, :, dcols] = sixteen(lambda p: dbuf[b, a, p])
        return carry

    lax.fori_loop(0, 16, last_columns, 0)
    for o in orders:
        for copy in o.bfar.values():
            copy.wait_recv()
    for k in range(0, width, 4096):
        span = pl.ds(k, 4096)
        left = hbuf[:, :, :, span].reshape(nq, 4096)
        for h in range(2):
            part = lax.dot_general(left, head_v[h, :, span], NT, preferred_element_type=F32)
            acc[h] = part.reshape(4, 4, 16, nv) + (acc[h] if k else 0.0)

    step = 512
    flat = [acc[h].reshape(nq, nv) for h in range(2)]
    peak = jnp.maximum(
        jnp.max(flat[0], axis=1, keepdims=True), jnp.max(flat[1], axis=1, keepdims=True)
    )
    sides = []
    denom = jnp.zeros((nq, 1), F32)
    for h in range(2):
        e = jnp.exp(flat[h] - peak)
        denom = denom + jnp.sum(e, axis=1, keepdims=True)
        hi = e.astype(BF16)
        low = (e - hi.astype(F32)).astype(BF16)
        sides.append(
            lax.dot_general(hi, w_v[h], NT, preferred_element_type=F32)
            + lax.dot_general(low, w_v[h], NT, preferred_element_type=F32)
        )
    both = sides[0] + sides[1]
    both = sum_terms(both[:, :128], both[:, 128:])
    is_peak = (lane >= 64) & (lane < 96)
    packed = jnp.where(first, both, jnp.where(is_peak, peak, denom))
    pm[:4] = packed.reshape(4, 4, 2, 8, 128)
    rcopies = [
        send(pm.at[:, a, b], rb1.at[k], rs.at[k], rr.at[k], r1dev[k])
        for k, (a, b) in enumerate(r1)
    ]

    l_pin.wait()

    def widths(i, carry):
        span = pl.ds(pl.multiple_of(i * step, step), step)
        left = hbuf[:, x, :, span].reshape(64, step)
        return carry + lax.dot_general(left, pin_v[:, span], NT, preferred_element_type=F32)

    w = lax.fori_loop(0, width // step, widths, jnp.zeros((64, 64), F32))
    wd[...] = jnp.concatenate([w, w], axis=1).reshape(4, 2, 8, 128)
    width2 = wd[:, zl].reshape(32, 128)

    def combine(parts):
        most = parts[0]
        for p in parts[1:]:
            most = jnp.maximum(most, p)
        m = most[:32, 64:65]
        sums, rows = None, None
        for p in parts:
            term = p[:32] * jnp.exp(p[:32, 64:65] - m)
            sums = term if sums is None else sums + term
            rows = p[32:] if rows is None else rows + p[32:]
        return jnp.concatenate([jnp.where(is_peak, most[:32], sums), rows], axis=0)

    def waited(copies, buf):
        got = []
        for k, copy in enumerate(copies):
            copy.wait_recv()
            got.append(buf[k].reshape(48, 128))
        return got

    mine = pm[:, x, zl].reshape(48, 128)
    mine = combine([mine] + waited(rcopies, rb1))
    rs2[...] = mine.reshape(6, 8, 128)
    rcopies = [send(rs2, rb2.at[k], rs.at[7 + k], rr.at[7 + k], to) for k, to in enumerate(r2dev)]
    mine = combine([mine] + waited(rcopies, rb2))
    rs3[...] = mine.reshape(6, 8, 128)
    rcopies = [send(rs3, rb3.at[k], rs.at[10 + k], rr.at[10 + k], to) for k, to in enumerate(r3dev)]
    mine = combine([mine] + waited(rcopies, rb3))

    tflat, mine = mine[32:], mine[:32]
    side = mine / mine[:, 96:97] - jnp.concatenate([tflat, pltpu.roll(tflat, 64, axis=1)], axis=0)
    for b in range(32):
        pair = jnp.where(first, side[:, 2 * b : 2 * b + 1], side[:, 2 * b + 1 : 2 * b + 2])
        kron[:, b * 128 : (b + 1) * 128] = (pair * width2).astype(BF16)
    l_store.wait()
    scores = lax.dot_general(kron[...], store_v[...], NT, preferred_element_type=F32)
    pairs = lax.broadcasted_iota(jnp.int32, (8, 1), 0) // 2
    for a in range(4):
        made = None
        for b in range(4):
            turned = scores[b * 8 : b * 8 + 8]
            if a != b:
                turned = pltpu.roll(turned, (2 * b - 2 * a) % 8, axis=0)
            made = turned if made is None else jnp.where(pairs == b, turned, made)
        out[a * 8 : a * 8 + 8] = made

    for copy in started:
        copy.wait_send()


def local(hidden_states, head, proj_out, proj_in, store, targets):
    nv, width = head.shape
    vm = pltpu.VMEM
    dma = pltpu.SemaphoreType.DMA
    return pl.pallas_call(
        kernel,
        out_shape=jax.ShapeDtypeStruct((32, 128), F32),
        in_specs=[pl.BlockSpec(memory_space=pltpu.HBM)] * 6,
        out_specs=pl.BlockSpec(memory_space=pltpu.VMEM),
        scratch_shapes=[
            vm((1, 512), jnp.int32),
            vm((8, 2, width), BF16),
            vm((4, 4, 16, width), BF16),
            vm((2, nv, width), BF16),
            vm((2, 64, nv), F32),
            vm((2, 256, nv), BF16),
            vm((64, width), BF16),
            vm((128, width), BF16),
            vm((2, 4, 4, 16, nv), F32),
            vm((6, 4, 2, 8, 128), F32),
            vm((7, 6, 8, 128), F32),
            vm((3, 6, 8, 128), F32),
            vm((3, 6, 8, 128), F32),
            vm((6, 8, 128), F32),
            vm((6, 8, 128), F32),
            vm((4, 2, 8, 128), F32),
            vm((32, width), BF16),
            dma((7,)), dma((2,)), dma((2,)), dma((7,)), dma((7,)),
            dma((40,)), dma((40,)), dma((13,)), dma((13,)),
            vm((4, 4, 8, 2, ZSHARE), BF16), dma((13,)), dma((13,)),
        ],
        compiler_params=pltpu.CompilerParams(
            collective_id=0, has_side_effects=True, vmem_limit_bytes=64 * 2**20 - 2**16
        ),
        cost_estimate=pl.CostEstimate(flops=2 * 10**9, bytes_accessed=10**7, transcendentals=0),
    )(hidden_states, head, proj_out.T, proj_in.T, store, targets.reshape(1, -1))

def solution(mesh):
    placed = (
        P(("vocab", "store"), None),
        P(("vocab", "store"), None),
        P(("vocab", "store"), None),
        P(),
        P("store", None),
        P(),
    )
    return jax.shard_map(
        local, mesh=mesh, in_specs=placed, out_specs=P("vocab", "store"), check_vma=False
    )
```

```python
import functools

import jax
import jax.numpy as jnp
from jax import lax
from jax.experimental import pallas as pl
from jax.experimental.pallas import tpu as pltpu
from jax.sharding import PartitionSpec as P

MESH = pl.DeviceIdType.MESH
ZSHARE = 768
F32 = jnp.float32
BF16 = jnp.bfloat16
NT = (((1,), (1,)), ((), ()))


def kernel(
    hid, head, po, pin, store, tgt, out,
    tgt_v, zbuf, hbuf, head_v, po_v, w_v, pin_v, store_v, acc,
    pm, rb1, rb2, rb3, rs2, rs3, wd, kron,
    lsem, csem_s, csem_r, zs, zr, gs, gr, ts, tr, rs, rr, dbuf, ds, dr,
):
    nv, width = head.shape
    v = lax.axis_index("vocab")
    s = lax.axis_index("store")
    c = lax.rem(v, 2)
    x = lax.rem(lax.div(v, 2), 4)
    zl = lax.div(v, 8)
    zh = lax.div(s, 4)
    y = lax.rem(s, 4)
    z = zh * 2 + zl

    def dev(x_, y_, zl_, zh_, c_=None):
        c_ = c if c_ is None else c_
        return ((zl_ * 4 + x_) * 2 + c_, zh_ * 4 + y_)

    def plus(a, d, n):
        return lax.rem(a + (d + n), n)

    peer = dev(x, y, zl, zh, 1 - c)
    zpeers = []
    for d in (4, 3, 5, 2, 6, 1, 7):
        zz = plus(z, d, 8)
        zpeers.append(dev(x, y, lax.rem(zz, 2), lax.div(zz, 2)))
    xpeer = {d: dev(plus(x, d, 4), y, zl, zh) for d in (-1, 1, 2)}
    ypeer = {d: dev(x, plus(y, d, 4), zl, zh) for d in (-1, 1, 2)}
    offs = [(2, 1), (1, 1), (3, 1), (2, 0), (1, 0), (3, 0), (0, 1)]
    r1 = [(plus(x, dx, 4), lax.rem(zl + dz, 2)) for dx, dz in offs]
    r1dev = [dev(a, y, b, zh) for a, b in r1]
    r2dev = [dev(x, plus(y, d, 4), zl, zh) for d in (2, 1, 3)]
    r3dev = [dev(x, y, zl, plus(zh, d, 4)) for d in (2, 1, 3)]

    l_hid = pltpu.make_async_copy(hid, zbuf.at[zl * 4 + zh], lsem.at[0])
    l_last = pltpu.make_async_copy(
        hid.at[:, pl.ds(width - ZSHARE, ZSHARE)], dbuf.at[y, x, zl * 4 + zh], lsem.at[6]
    )
    l_po = pltpu.make_async_copy(po, po_v.at[0], lsem.at[1])
    l_head = pltpu.make_async_copy(head, head_v.at[0], lsem.at[2])
    l_pin = pltpu.make_async_copy(pin, pin_v, lsem.at[3])
    l_store = pltpu.make_async_copy(store, store_v, lsem.at[4])
    l_tgt = pltpu.make_async_copy(tgt, tgt_v, lsem.at[5])
    for l in (l_hid, l_last, l_po, l_tgt, l_head, l_pin, l_store):
        l.start()

    barrier = pltpu.get_barrier_semaphore()
    greet = zpeers + [dev(plus(x, d, 4), y, zl, zh) for d in (1, 2, 3)] + r2dev
    greet += [r1dev[k] for k, (dx, dz) in enumerate(offs) if dz and dx] + [peer]
    for other in greet:
        pl.semaphore_signal(barrier, inc=1, device_id=other, device_id_type=MESH)
    pl.semaphore_wait(barrier, len(greet))

    zcols = ZSHARE
    half = (width - zcols) // 2
    xycols, dcols = pl.ds(0, 2 * half), pl.ds(2 * half, zcols)

    started = []

    def send(src, dst, ssem, rsem, to):
        copy = pltpu.make_async_remote_copy(
            src_ref=src, dst_ref=dst, send_sem=ssem, recv_sem=rsem,
            device_id=to, device_id_type=MESH,
        )
        copy.start()
        started.append(copy)
        return copy

    here = zl * 4 + zh
    l_hid.wait()
    l_last.wait()
    zcopies = [
        send(zbuf.at[here, :, xycols], zbuf.at[here, :, xycols], zs.at[k], zr.at[k], to)
        for k, to in enumerate(zpeers)
    ]
    xall = [xpeer[d] for d in (2, 1, -1)]
    yall = [ypeer[d] for d in (2, 1, -1)]
    dxs = [
        send(dbuf.at[y, x, here], dbuf.at[y, x, here], ds.at[k], dr.at[k], to)
        for k, to in enumerate(xall)
    ]
    c_po = send(po, po_v.at[1], csem_s.at[0], csem_r.at[0], peer)
    c_head = send(head, head_v.at[1], csem_s.at[1], csem_r.at[1], peer)

    def split(h):
        p = po_v[h]
        hi = p.astype(BF16).astype(F32)
        rest = p - hi
        mid = rest.astype(BF16).astype(F32)
        low = rest - mid
        w_v[h] = jnp.concatenate([hi, mid, low, jnp.zeros_like(p)], axis=0).astype(BF16)

    lane = lax.broadcasted_iota(jnp.int32, (1, 128), 1)
    first = lane < 64

    nq = 256
    row = lax.broadcasted_iota(jnp.int32, (nq, 1), 0)
    ry, rx, rzl, rzh, ri = (
        row // 64, (row // 16) % 4, (row // 8) % 2, (row // 2) % 4, row % 2,
    )
    query = 2 * (((rzl * 4 + rx) * 2 + c) * 16 + rzh * 4 + ry) + ri
    ids = lax.broadcasted_iota(jnp.int32, (1, 512), 1)
    l_tgt.wait()
    wanted = jnp.sum(
        jnp.where(ids == query, tgt_v[...].astype(F32), 0.0), axis=1, keepdims=True
    )

    def sum_terms(a, b):
        half = a + pltpu.roll(a, 64, axis=1)
        return half + (b + pltpu.roll(b, 64, axis=1))

    def target_rows(h):
        base = (((v - c) + lax.rem(c + h, 2)) * 16 + s) * nv
        cols = (lax.broadcasted_iota(jnp.int32, (1, nv), 1) + base).astype(F32)
        hot = jnp.where(cols == wanted, 1.0, 0.0).astype(BF16)
        return lax.dot_general(hot, w_v[h], NT, preferred_element_type=F32)

    l_po.wait()
    split(0)
    t0 = target_rows(0)
    c_po.wait_recv()
    split(1)
    t01 = t0 + target_rows(1)
    t = sum_terms(t01[:, :128], t01[:, 128:]).reshape(4, 64, 128)
    pm[4:] = jnp.where(first, t[:2], t[2:]).reshape(2, 4, 2, 8, 128)
    for copy in dxs:
        copy.wait_recv()
    dcolumn = dbuf.at[y, :, here]
    dys = [send(dcolumn, dcolumn, ds.at[3 + k], dr.at[3 + k], to) for k, to in enumerate(yall)]
    for k in zcopies:
        k.wait_recv()
    rows8 = lax.broadcasted_iota(jnp.int32, (8, 1), 0)

    def sixteen(piece):
        halves = []
        for tile in range(2):
            made = None
            for p in range(4):
                pair = piece(tile * 4 + p).astype(F32)
                for i in range(2):
                    row_ = jnp.broadcast_to(pair[i : i + 1], (8, pair.shape[1]))
                    made = row_ if made is None else jnp.where(rows8 == 2 * p + i, row_, made)
            halves.append(made)
        return jnp.concatenate(halves, axis=0).astype(BF16)

    quarter = (half // 256) * 128

    class Order:
        def __init__(self, base, sem, apeer, bpeer, block):
            self.cols = pl.ds(base, half)
            self.part = {1: pl.ds(base, quarter), -1: pl.ds(base + quarter, half - quarter)}
            self.sem, self.apeer, self.bpeer, self.block = sem, apeer, bpeer, block
            self.near, self.bnear, self.bfar = {}, {}, {}

        def put(self, j, block, cols, to):
            view = hbuf.at[block[0], block[1], :, cols]
            return send(view, view, gs.at[self.sem + j], gr.at[self.sem + j], to)

        def own(self):
            for k, d in enumerate((1, -1, 2)):
                self.near[d] = self.put(k, self.block(0, 0), self.cols, self.apeer[d])

        def onward(self, j, da):
            for k, d in enumerate((1, -1)):
                self.bnear[da, d] = self.put(4 + j * 2 + k, self.block(da, 0), self.cols, self.bpeer[d])
            if j in (2, 3,):
                self.bfar[da, 2] = self.put(12 + j * 2, self.block(da, 0), self.cols, self.bpeer[2])

        def bpass_on(self, j, da):
            for k, d in enumerate((1, -1)):
                self.bnear[da, d].wait_recv()
                if j in (2, 3,):
                    continue
                self.bfar[da, d] = self.put(12 + j * 2 + k, self.block(da, -d), self.part[d], self.bpeer[d])

    orders = [
        Order(0, 0, xpeer, ypeer, lambda a, b: (plus(y, b, 4), plus(x, a, 4))),
        Order(half, 20, ypeer, xpeer, lambda a, b: (plus(y, a, 4), plus(x, b, 4))),
    ]
    for o, base in zip(orders, (0, half)):
        for n in range(base, base + half, half // 2 // 128 * 128):
            span = pl.ds(n, min(half // 2 // 128 * 128, base + half - n))
            hbuf[y, x, :, span] = sixteen(lambda p: zbuf[p, :, span])
        o.own()
    for o in orders:
        o.onward(0, 0)
    for copy in dys:
        copy.wait_recv()
    dplane = dbuf.at[:, :, here]
    dzs = [
        send(dplane, dplane, ds.at[6 + k], dr.at[6 + k], to) for k, to in enumerate(zpeers)
    ]
    for k, d in enumerate((1, -1)):
        for o in orders:
            o.near[d].wait_recv()
            o.onward(1 + k, -d)

    for o in orders:
        o.near[2].wait_recv()
        o.onward(3, 2)
    for o in orders:
        o.bpass_on(0, 0)
    for k, d in enumerate((1, -1)):
        for o in orders:
            o.bpass_on(1 + k, -d)

    l_head.wait()
    c_head.wait_recv()

    for o in orders:
        o.bpass_on(3, 2)
    for copy in dzs:
        copy.wait_recv()

    def last_columns(k, carry):
        b, a = lax.div(k, 4), lax.rem(k, 4)
        hbuf[b, a, :, dcols] = sixteen(lambda p: dbuf[b, a, p])
        return carry

    lax.fori_loop(0, 16, last_columns, 0)
    for o in orders:
        for copy in o.bfar.values():
            copy.wait_recv()
    tcopies = [
        send(pm.at[pl.ds(4, 2), a, b], rb1.at[k, pl.ds(4, 2)], ts.at[k], tr.at[k], r1dev[k])
        for k, (a, b) in enumerate(r1)
    ]
    left = hbuf[...].reshape(nq, width)
    for h in range(2):
        part = lax.dot_general(left, head_v[h], NT, preferred_element_type=F32)
        acc[h] = part.reshape(4, 4, 16, nv)

    step = 512
    flat = [acc[h].reshape(nq, nv) for h in range(2)]
    peak = jnp.maximum(
        jnp.max(flat[0], axis=1, keepdims=True), jnp.max(flat[1], axis=1, keepdims=True)
    )
    sides = []
    denom = jnp.zeros((nq, 1), F32)
    for h in range(2):
        e = jnp.exp(flat[h] - peak)
        denom = denom + jnp.sum(e, axis=1, keepdims=True)
        hi = e.astype(BF16)
        low = (e - hi.astype(F32)).astype(BF16)
        sides.append(
            lax.dot_general(hi, w_v[h], NT, preferred_element_type=F32)
            + lax.dot_general(low, w_v[h], NT, preferred_element_type=F32)
        )
    both = sides[0] + sides[1]
    both = sum_terms(both[:, :128], both[:, 128:])
    is_peak = (lane >= 64) & (lane < 96)
    packed = jnp.where(first, both, jnp.where(is_peak, peak, denom))
    pm[:4] = packed.reshape(4, 4, 2, 8, 128)
    rcopies = [
        send(
            pm.at[pl.ds(0, 4), a, b], rb1.at[k, pl.ds(0, 4)], rs.at[k], rr.at[k], r1dev[k]
        )
        for k, (a, b) in enumerate(r1)
    ]

    l_pin.wait()

    def widths(i, carry):
        span = pl.ds(pl.multiple_of(i * step, step), step)
        left = hbuf[:, x, :, span].reshape(64, step)
        return carry + lax.dot_general(left, pin_v[:, span], NT, preferred_element_type=F32)

    w = lax.fori_loop(0, width // step, widths, jnp.zeros((64, 64), F32))
    wd[...] = jnp.concatenate([w, w], axis=1).reshape(4, 2, 8, 128)
    width2 = wd[:, zl].reshape(32, 128)

    def combine(parts):
        most = parts[0]
        for p in parts[1:]:
            most = jnp.maximum(most, p)
        m = most[:32, 64:65]
        sums, rows = None, None
        for p in parts:
            term = p[:32] * jnp.exp(p[:32, 64:65] - m)
            sums = term if sums is None else sums + term
            rows = p[32:] if rows is None else rows + p[32:]
        return jnp.concatenate([jnp.where(is_peak, most[:32], sums), rows], axis=0)

    def waited(copies, buf):
        got = []
        for k, copy in enumerate(copies):
            copy.wait_recv()
            got.append(buf[k].reshape(48, 128))
        return got

    for copy in tcopies:
        copy.wait_recv()
    mine = pm[:, x, zl].reshape(48, 128)
    mine = combine([mine] + waited(rcopies, rb1))
    rs2[...] = mine.reshape(6, 8, 128)
    rcopies = [send(rs2, rb2.at[k], rs.at[7 + k], rr.at[7 + k], to) for k, to in enumerate(r2dev)]
    mine = combine([mine] + waited(rcopies, rb2))
    rs3[...] = mine.reshape(6, 8, 128)
    rcopies = [send(rs3, rb3.at[k], rs.at[10 + k], rr.at[10 + k], to) for k, to in enumerate(r3dev)]
    mine = combine([mine] + waited(rcopies, rb3))

    tflat, mine = mine[32:], mine[:32]
    side = mine / mine[:, 96:97] - jnp.concatenate([tflat, pltpu.roll(tflat, 64, axis=1)], axis=0)
    for b in range(32):
        pair = jnp.where(first, side[:, 2 * b : 2 * b + 1], side[:, 2 * b + 1 : 2 * b + 2])
        kron[:, b * 128 : (b + 1) * 128] = (pair * width2).astype(BF16)
    l_store.wait()
    scores = lax.dot_general(kron[...], store_v[...], NT, preferred_element_type=F32)
    pairs = lax.broadcasted_iota(jnp.int32, (8, 1), 0) // 2
    for a in range(4):
        made = None
        for b in range(4):
            turned = scores[b * 8 : b * 8 + 8]
            if a != b:
                turned = pltpu.roll(turned, (2 * b - 2 * a) % 8, axis=0)
            made = turned if made is None else jnp.where(pairs == b, turned, made)
        out[a * 8 : a * 8 + 8] = made

    for copy in started:
        copy.wait_send()


def local(hidden_states, head, proj_out, proj_in, store, targets):
    nv, width = head.shape
    vm = pltpu.VMEM
    dma = pltpu.SemaphoreType.DMA
    return pl.pallas_call(
        kernel,
        out_shape=jax.ShapeDtypeStruct((32, 128), F32),
        in_specs=[pl.BlockSpec(memory_space=pltpu.HBM)] * 6,
        out_specs=pl.BlockSpec(memory_space=pltpu.VMEM),
        scratch_shapes=[
            vm((1, 512), jnp.int32),
            vm((8, 2, width), BF16),
            vm((4, 4, 16, width), BF16),
            vm((2, nv, width), BF16),
            vm((2, 64, nv), F32),
            vm((2, 256, nv), BF16),
            vm((64, width), BF16),
            vm((128, width), BF16),
            vm((2, 4, 4, 16, nv), F32),
            vm((6, 4, 2, 8, 128), F32),
            vm((7, 6, 8, 128), F32),
            vm((3, 6, 8, 128), F32),
            vm((3, 6, 8, 128), F32),
            vm((6, 8, 128), F32),
            vm((6, 8, 128), F32),
            vm((4, 2, 8, 128), F32),
            vm((32, width), BF16),
            dma((7,)), dma((2,)), dma((2,)), dma((7,)), dma((7,)),
            dma((40,)), dma((40,)), dma((7,)), dma((7,)), dma((13,)), dma((13,)),
            vm((4, 4, 8, 2, ZSHARE), BF16), dma((13,)), dma((13,)),
        ],
        compiler_params=pltpu.CompilerParams(
            collective_id=0, has_side_effects=True, vmem_limit_bytes=64 * 2**20 - 2**16
        ),
        cost_estimate=pl.CostEstimate(flops=2 * 10**9, bytes_accessed=10**7, transcendentals=0),
    )(hidden_states, head, proj_out.T, proj_in.T, store, targets.reshape(1, -1))

def solution(mesh):
    placed = (
        P(("vocab", "store"), None),
        P(("vocab", "store"), None),
        P(("vocab", "store"), None),
        P(),
        P("store", None),
        P(),
    )
    return jax.shard_map(
        local, mesh=mesh, in_specs=placed, out_specs=P("vocab", "store"), check_vma=False
    )
```

```python
import functools

import jax
import jax.numpy as jnp
from jax import lax
from jax.experimental import pallas as pl
from jax.experimental.pallas import tpu as pltpu
from jax.sharding import PartitionSpec as P

MESH = pl.DeviceIdType.MESH
ZSHARE = 768
F32 = jnp.float32
BF16 = jnp.bfloat16
NT = (((1,), (1,)), ((), ()))


def kernel(
    hid, head, po, pin, store, tgt, out,
    tgt_v, zbuf, hbuf, head_v, po_v, w_v, pin_v, store_v, acc,
    pm, rb1, rb2, rb3, rs2, rs3, wd, kron,
    lsem, csem_s, csem_r, zs, zr, gs, gr, ts, tr, rs, rr, dbuf, ds, dr,
):
    nv, width = head.shape
    v = lax.axis_index("vocab")
    s = lax.axis_index("store")
    c = lax.rem(v, 2)
    x = lax.rem(lax.div(v, 2), 4)
    zl = lax.div(v, 8)
    zh = lax.div(s, 4)
    y = lax.rem(s, 4)
    z = zh * 2 + zl

    def dev(x_, y_, zl_, zh_, c_=None):
        c_ = c if c_ is None else c_
        return ((zl_ * 4 + x_) * 2 + c_, zh_ * 4 + y_)

    def plus(a, d, n):
        return lax.rem(a + (d + n), n)

    peer = dev(x, y, zl, zh, 1 - c)
    zpeers = []
    for d in (4, 3, 5, 2, 6, 1, 7):
        zz = plus(z, d, 8)
        zpeers.append(dev(x, y, lax.rem(zz, 2), lax.div(zz, 2)))
    xpeer = {d: dev(plus(x, d, 4), y, zl, zh) for d in (-1, 1, 2)}
    ypeer = {d: dev(x, plus(y, d, 4), zl, zh) for d in (-1, 1, 2)}
    offs = [(2, 1), (1, 1), (3, 1), (2, 0), (1, 0), (3, 0), (0, 1)]
    r1 = [(plus(x, dx, 4), lax.rem(zl + dz, 2)) for dx, dz in offs]
    r1dev = [dev(a, y, b, zh) for a, b in r1]
    r2dev = [dev(x, plus(y, d, 4), zl, zh) for d in (2, 1, 3)]
    r3dev = [dev(x, y, zl, plus(zh, d, 4)) for d in (2, 1, 3)]

    barrier = pltpu.get_barrier_semaphore()
    greet = zpeers + [dev(plus(x, d, 4), y, zl, zh) for d in (1, 2, 3)] + r2dev
    greet += [r1dev[k] for k, (dx, dz) in enumerate(offs) if dz and dx] + [peer]
    for other in greet:
        pl.semaphore_signal(barrier, inc=1, device_id=other, device_id_type=MESH)
    l_hid = pltpu.make_async_copy(hid, zbuf.at[zl * 4 + zh], lsem.at[0])
    l_last = pltpu.make_async_copy(
        hid.at[:, pl.ds(width - ZSHARE, ZSHARE)], dbuf.at[y, x, zl * 4 + zh], lsem.at[6]
    )
    l_po = pltpu.make_async_copy(po, po_v.at[0], lsem.at[1])
    l_head = pltpu.make_async_copy(head, head_v.at[0], lsem.at[2])
    l_pin = pltpu.make_async_copy(pin, pin_v, lsem.at[3])
    l_store = pltpu.make_async_copy(store, store_v, lsem.at[4])
    l_tgt = pltpu.make_async_copy(tgt, tgt_v, lsem.at[5])
    for l in (l_hid, l_last, l_po, l_tgt, l_head, l_pin, l_store):
        l.start()

    pl.semaphore_wait(barrier, len(greet))

    zcols = ZSHARE
    half = (width - zcols) // 2
    xycols, dcols = pl.ds(0, 2 * half), pl.ds(2 * half, zcols)

    started = []

    def send(src, dst, ssem, rsem, to):
        copy = pltpu.make_async_remote_copy(
            src_ref=src, dst_ref=dst, send_sem=ssem, recv_sem=rsem,
            device_id=to, device_id_type=MESH,
        )
        copy.start()
        started.append(copy)
        return copy

    here = zl * 4 + zh
    l_hid.wait()
    l_last.wait()
    zcopies = [
        send(zbuf.at[here, :, xycols], zbuf.at[here, :, xycols], zs.at[k], zr.at[k], to)
        for k, to in enumerate(zpeers)
    ]
    xall = [xpeer[d] for d in (2, 1, -1)]
    yall = [ypeer[d] for d in (2, 1, -1)]
    dxs = [
        send(dbuf.at[y, x, here], dbuf.at[y, x, here], ds.at[k], dr.at[k], to)
        for k, to in enumerate(xall)
    ]
    c_po = send(po, po_v.at[1], csem_s.at[0], csem_r.at[0], peer)
    c_head = send(head, head_v.at[1], csem_s.at[1], csem_r.at[1], peer)

    def split(h):
        p = po_v[h]
        hi = p.astype(BF16).astype(F32)
        rest = p - hi
        mid = rest.astype(BF16).astype(F32)
        low = rest - mid
        w_v[h] = jnp.concatenate([hi, mid, low, jnp.zeros_like(p)], axis=0).astype(BF16)

    lane = lax.broadcasted_iota(jnp.int32, (1, 128), 1)
    first = lane < 64

    nq = 256
    row = lax.broadcasted_iota(jnp.int32, (nq, 1), 0)
    ry, rx, rzl, rzh, ri = (
        row // 64, (row // 16) % 4, (row // 8) % 2, (row // 2) % 4, row % 2,
    )
    query = 2 * (((rzl * 4 + rx) * 2 + c) * 16 + rzh * 4 + ry) + ri
    ids = lax.broadcasted_iota(jnp.int32, (1, 512), 1)
    l_tgt.wait()
    wanted = jnp.sum(
        jnp.where(ids == query, tgt_v[...].astype(F32), 0.0), axis=1, keepdims=True
    )

    def sum_terms(a, b):
        half = a + pltpu.roll(a, 64, axis=1)
        return half + (b + pltpu.roll(b, 64, axis=1))

    def target_rows(h):
        base = (((v - c) + lax.rem(c + h, 2)) * 16 + s) * nv
        cols = (lax.broadcasted_iota(jnp.int32, (1, nv), 1) + base).astype(F32)
        hot = jnp.where(cols == wanted, 1.0, 0.0).astype(BF16)
        return lax.dot_general(hot, w_v[h], NT, preferred_element_type=F32)

    l_po.wait()
    split(0)
    t0 = target_rows(0)
    c_po.wait_recv()
    split(1)
    t01 = t0 + target_rows(1)
    t = sum_terms(t01[:, :128], t01[:, 128:]).reshape(4, 64, 128)
    t = jnp.where(first, t[:2], t[2:]).reshape(2, 4, 2, 8, 128)
    for k in range(2):
        pm[:, :, 4 + k] = t[k]
    for copy in dxs:
        copy.wait_recv()
    dcolumn = dbuf.at[y, :, here]
    dys = [send(dcolumn, dcolumn, ds.at[3 + k], dr.at[3 + k], to) for k, to in enumerate(yall)]
    for k in zcopies:
        k.wait_recv()
    rows8 = lax.broadcasted_iota(jnp.int32, (8, 1), 0)

    def sixteen(piece):
        halves = []
        for tile in range(2):
            made = None
            for p in range(4):
                pair = piece(tile * 4 + p).astype(F32)
                for i in range(2):
                    row_ = jnp.broadcast_to(pair[i : i + 1], (8, pair.shape[1]))
                    made = row_ if made is None else jnp.where(rows8 == 2 * p + i, row_, made)
            halves.append(made)
        return jnp.concatenate(halves, axis=0).astype(BF16)

    quarter = (half // 256) * 128

    class Order:
        def __init__(self, base, sem, apeer, bpeer, block):
            self.cols = pl.ds(base, half)
            self.part = {1: pl.ds(base, quarter), -1: pl.ds(base + quarter, half - quarter)}
            self.sem, self.apeer, self.bpeer, self.block = sem, apeer, bpeer, block
            self.near, self.bnear, self.bfar = {}, {}, {}

        def put(self, j, block, cols, to):
            view = hbuf.at[block[0], block[1], :, cols]
            return send(view, view, gs.at[self.sem + j], gr.at[self.sem + j], to)

        def own(self):
            for k, d in enumerate((1, -1, 2)):
                self.near[d] = self.put(k, self.block(0, 0), self.cols, self.apeer[d])

        def onward(self, j, da):
            for k, d in enumerate((1, -1)):
                self.bnear[da, d] = self.put(4 + j * 2 + k, self.block(da, 0), self.cols, self.bpeer[d])
            if j in (2, 3,):
                self.bfar[da, 2] = self.put(12 + j * 2, self.block(da, 0), self.cols, self.bpeer[2])

        def bpass_on(self, j, da):
            for k, d in enumerate((1, -1)):
                self.bnear[da, d].wait_recv()
                if j in (2, 3,):
                    continue
                self.bfar[da, d] = self.put(12 + j * 2 + k, self.block(da, -d), self.part[d], self.bpeer[d])

    orders = [
        Order(0, 0, xpeer, ypeer, lambda a, b: (plus(y, b, 4), plus(x, a, 4))),
        Order(half, 20, ypeer, xpeer, lambda a, b: (plus(y, a, 4), plus(x, b, 4))),
    ]
    for o, base in zip(orders, (0, half)):
        for n in range(base, base + half, half // 2 // 128 * 128):
            span = pl.ds(n, min(half // 2 // 128 * 128, base + half - n))
            hbuf[y, x, :, span] = sixteen(lambda p: zbuf[p, :, span])
        o.own()
    for o in orders:
        o.onward(0, 0)
    for copy in dys:
        copy.wait_recv()
    dplane = dbuf.at[:, :, here]
    dzs = [
        send(dplane, dplane, ds.at[6 + k], dr.at[6 + k], to) for k, to in enumerate(zpeers)
    ]
    for k, d in enumerate((1, -1)):
        for o in orders:
            o.near[d].wait_recv()
            o.onward(1 + k, -d)

    for o in orders:
        o.near[2].wait_recv()
        o.onward(3, 2)
    for o in orders:
        o.bpass_on(0, 0)
    for k, d in enumerate((1, -1)):
        for o in orders:
            o.bpass_on(1 + k, -d)

    l_head.wait()
    c_head.wait_recv()

    for o in orders:
        o.bpass_on(3, 2)
    for copy in dzs:
        copy.wait_recv()

    def last_columns(k, carry):
        b, a = lax.div(k, 4), lax.rem(k, 4)
        hbuf[b, a, :, dcols] = sixteen(lambda p: dbuf[b, a, p])
        return carry

    lax.fori_loop(0, 16, last_columns, 0)
    for o in orders:
        for copy in o.bfar.values():
            copy.wait_recv()
    tcopies = [
        send(pm.at[a, b, pl.ds(4, 2)], rb1.at[k, pl.ds(4, 2)], ts.at[k], tr.at[k], r1dev[k])
        for k, (a, b) in enumerate(r1)
    ]
    left = hbuf[...].reshape(nq, width)
    for h in range(2):
        part = lax.dot_general(left, head_v[h], NT, preferred_element_type=F32)
        acc[h] = part.reshape(4, 4, 16, nv)

    step = 512
    flat = [acc[h].reshape(nq, nv) for h in range(2)]
    peak = jnp.maximum(
        jnp.max(flat[0], axis=1, keepdims=True), jnp.max(flat[1], axis=1, keepdims=True)
    )
    sides = []
    denom = jnp.zeros((nq, 1), F32)
    for h in range(2):
        e = jnp.exp(flat[h] - peak)
        denom = denom + jnp.sum(e, axis=1, keepdims=True)
        hi = e.astype(BF16)
        low = (e - hi.astype(F32)).astype(BF16)
        sides.append(
            lax.dot_general(hi, w_v[h], NT, preferred_element_type=F32)
            + lax.dot_general(low, w_v[h], NT, preferred_element_type=F32)
        )
    both = sides[0] + sides[1]
    both = sum_terms(both[:, :128], both[:, 128:])
    is_peak = (lane >= 64) & (lane < 96)
    packed = jnp.where(first, both, jnp.where(is_peak, peak, denom))
    packed = packed.reshape(4, 4, 2, 8, 128)
    for k in range(4):
        pm[:, :, k] = packed[k]
    rcopies = [
        send(
            pm.at[a, b, pl.ds(0, 4)], rb1.at[k, pl.ds(0, 4)], rs.at[k], rr.at[k], r1dev[k]
        )
        for k, (a, b) in enumerate(r1)
    ]

    l_pin.wait()

    def widths(i, carry):
        span = pl.ds(pl.multiple_of(i * step, step), step)
        left = hbuf[:, x, :, span].reshape(64, step)
        return carry + lax.dot_general(left, pin_v[:, span], NT, preferred_element_type=F32)

    w = lax.fori_loop(0, width // step, widths, jnp.zeros((64, 64), F32))
    wd[...] = jnp.concatenate([w, w], axis=1).reshape(4, 2, 8, 128)
    width2 = wd[:, zl].reshape(32, 128)

    def combine(parts):
        most = parts[0]
        for p in parts[1:]:
            most = jnp.maximum(most, p)
        m = most[:, 64:65]
        sums = None
        for p in parts:
            term = p * jnp.exp(p[:, 64:65] - m)
            sums = term if sums is None else sums + term
        return jnp.where(is_peak, most, sums)

    def waited(copies, buf):
        got = []
        for k, copy in enumerate(copies):
            copy.wait_recv()
            got.append(buf[k, :4].reshape(32, 128))
        return got

    def target_sum(total, copies, buf):
        for k, copy in enumerate(copies):
            copy.wait_recv()
            total = total + buf[k, 4:].reshape(16, 128)
        return total

    sums_of, rows_of = pl.ds(0, 4), pl.ds(4, 2)

    def step_on(held, bufs, first_sem, sems, part, to_all):
        return [
            send(held.at[part], bufs.at[k, part], sems[0].at[first_sem + k], sems[1].at[first_sem + k], to)
            for k, to in enumerate(to_all)
        ]

    rows = target_sum(pm[x, zl, 4:].reshape(16, 128), tcopies, rb1)
    rs2[4:] = rows.reshape(2, 8, 128)
    tcopies = step_on(rs2, rb2, 7, (ts, tr), rows_of, r2dev)
    mine = pm[x, zl, :4].reshape(32, 128)
    mine = combine([mine] + waited(rcopies, rb1))
    rs2[:4] = mine.reshape(4, 8, 128)
    rcopies = step_on(rs2, rb2, 7, (rs, rr), sums_of, r2dev)
    rows = target_sum(rows, tcopies, rb2)
    rs3[4:] = rows.reshape(2, 8, 128)
    tcopies = step_on(rs3, rb3, 10, (ts, tr), rows_of, r3dev)
    mine = combine([mine] + waited(rcopies, rb2))
    rs3[:4] = mine.reshape(4, 8, 128)
    rcopies = step_on(rs3, rb3, 10, (rs, rr), sums_of, r3dev)
    rows = target_sum(rows, tcopies, rb3)
    mine = combine([mine] + waited(rcopies, rb3))

    side = mine / mine[:, 96:97] - jnp.concatenate([rows, pltpu.roll(rows, 64, axis=1)], axis=0)
    for b in range(32):
        pair = jnp.where(first, side[:, 2 * b : 2 * b + 1], side[:, 2 * b + 1 : 2 * b + 2])
        kron[:, b * 128 : (b + 1) * 128] = (pair * width2).astype(BF16)
    l_store.wait()
    scores = lax.dot_general(kron[...], store_v[...], NT, preferred_element_type=F32)
    pairs = lax.broadcasted_iota(jnp.int32, (8, 1), 0) // 2
    for a in range(4):
        made = None
        for b in range(4):
            turned = scores[b * 8 : b * 8 + 8]
            if a != b:
                turned = pltpu.roll(turned, (2 * b - 2 * a) % 8, axis=0)
            made = turned if made is None else jnp.where(pairs == b, turned, made)
        out[a * 8 : a * 8 + 8] = made

    for copy in started:
        copy.wait_send()


def local(hidden_states, head, proj_out, proj_in, store, targets):
    nv, width = head.shape
    vm = pltpu.VMEM
    dma = pltpu.SemaphoreType.DMA
    return pl.pallas_call(
        kernel,
        out_shape=jax.ShapeDtypeStruct((32, 128), F32),
        in_specs=[pl.BlockSpec(memory_space=pltpu.HBM)] * 6,
        out_specs=pl.BlockSpec(memory_space=pltpu.VMEM),
        scratch_shapes=[
            vm((1, 512), jnp.int32),
            vm((8, 2, width), BF16),
            vm((4, 4, 16, width), BF16),
            vm((2, nv, width), BF16),
            vm((2, 64, nv), F32),
            vm((2, 256, nv), BF16),
            vm((64, width), BF16),
            vm((128, width), BF16),
            vm((2, 4, 4, 16, nv), F32),
            vm((4, 2, 6, 8, 128), F32),
            vm((7, 6, 8, 128), F32),
            vm((3, 6, 8, 128), F32),
            vm((3, 6, 8, 128), F32),
            vm((6, 8, 128), F32),
            vm((6, 8, 128), F32),
            vm((4, 2, 8, 128), F32),
            vm((32, width), BF16),
            dma((7,)), dma((2,)), dma((2,)), dma((7,)), dma((7,)),
            dma((40,)), dma((40,)), dma((13,)), dma((13,)), dma((13,)), dma((13,)),
            vm((4, 4, 8, 2, ZSHARE), BF16), dma((13,)), dma((13,)),
        ],
        compiler_params=pltpu.CompilerParams(
            collective_id=0, has_side_effects=True, vmem_limit_bytes=64 * 2**20 - 2**16
        ),
        cost_estimate=pl.CostEstimate(flops=2 * 10**9, bytes_accessed=10**7, transcendentals=0),
    )(hidden_states, head, proj_out.T, proj_in.T, store, targets.reshape(1, -1))

def solution(mesh):
    placed = (
        P(("vocab", "store"), None),
        P(("vocab", "store"), None),
        P(("vocab", "store"), None),
        P(),
        P("store", None),
        P(),
    )
    return jax.shard_map(
        local, mesh=mesh, in_specs=placed, out_specs=P("vocab", "store"), check_vma=False
    )
```

```python
import functools

import jax
import jax.numpy as jnp
from jax import lax
from jax.experimental import pallas as pl
from jax.experimental.pallas import tpu as pltpu
from jax.sharding import PartitionSpec as P

MESH = pl.DeviceIdType.MESH
ZSHARE = 768
F32 = jnp.float32
BF16 = jnp.bfloat16
NT = (((1,), (1,)), ((), ()))


def kernel(
    hid, head, po, pin, store, tgt, out,
    tgt_v, zbuf, hbuf, head_v, po_v, w_v, pin_v, store_v, acc,
    pm, rb1, rb2, rb3, rs2, rs3, wd, kron,
    lsem, csem_s, csem_r, zs, zr, gs, gr, ts, tr, rs, rr, dbuf, ds, dr,
):
    nv, width = head.shape
    v = lax.axis_index("vocab")
    s = lax.axis_index("store")
    c = lax.rem(v, 2)
    x = lax.rem(lax.div(v, 2), 4)
    zl = lax.div(v, 8)
    zh = lax.div(s, 4)
    y = lax.rem(s, 4)
    z = zh * 2 + zl

    def dev(x_, y_, zl_, zh_, c_=None):
        c_ = c if c_ is None else c_
        return ((zl_ * 4 + x_) * 2 + c_, zh_ * 4 + y_)

    def plus(a, d, n):
        return lax.rem(a + (d + n), n)

    peer = dev(x, y, zl, zh, 1 - c)
    zpeers = []
    for d in (4, 3, 5, 2, 6, 1, 7):
        zz = plus(z, d, 8)
        zpeers.append(dev(x, y, lax.rem(zz, 2), lax.div(zz, 2)))
    xpeer = {d: dev(plus(x, d, 4), y, zl, zh) for d in (-1, 1, 2)}
    ypeer = {d: dev(x, plus(y, d, 4), zl, zh) for d in (-1, 1, 2)}
    offs = [(2, 1), (1, 1), (3, 1), (2, 0), (1, 0), (3, 0), (0, 1)]
    r1 = [(plus(x, dx, 4), lax.rem(zl + dz, 2)) for dx, dz in offs]
    r1dev = [dev(a, y, b, zh) for a, b in r1]
    r2dev = [dev(x, plus(y, d, 4), zl, zh) for d in (2, 1, 3)]
    r3dev = [dev(x, y, zl, plus(zh, d, 4)) for d in (2, 1, 3)]

    barrier = pltpu.get_barrier_semaphore()
    greet = zpeers + [dev(plus(x, d, 4), y, zl, zh) for d in (1, 2, 3)] + r2dev
    greet += [r1dev[k] for k, (dx, dz) in enumerate(offs) if dz and dx] + [peer]
    for other in greet:
        pl.semaphore_signal(barrier, inc=1, device_id=other, device_id_type=MESH)
    l_hid = pltpu.make_async_copy(hid, zbuf.at[zl * 4 + zh], lsem.at[0])
    l_last = pltpu.make_async_copy(
        hid.at[:, pl.ds(width - ZSHARE, ZSHARE)], dbuf.at[y, x, zl * 4 + zh], lsem.at[6]
    )
    l_po = pltpu.make_async_copy(po, po_v.at[0], lsem.at[1])
    l_head = pltpu.make_async_copy(head, head_v.at[0], lsem.at[2])
    l_pin = pltpu.make_async_copy(pin, pin_v, lsem.at[3])
    l_store = pltpu.make_async_copy(store, store_v, lsem.at[4])
    l_tgt = pltpu.make_async_copy(tgt, tgt_v, lsem.at[5])
    for l in (l_hid, l_last, l_po, l_tgt):
        l.start()

    pl.semaphore_wait(barrier, len(greet))

    zcols = ZSHARE
    half = (width - zcols) // 2
    xycols, dcols = pl.ds(0, 2 * half), pl.ds(2 * half, zcols)

    started = []

    def send(src, dst, ssem, rsem, to):
        copy = pltpu.make_async_remote_copy(
            src_ref=src, dst_ref=dst, send_sem=ssem, recv_sem=rsem,
            device_id=to, device_id_type=MESH,
        )
        copy.start()
        started.append(copy)
        return copy

    here = zl * 4 + zh
    l_hid.wait()
    l_last.wait()
    zcopies = [
        send(zbuf.at[here, :, xycols], zbuf.at[here, :, xycols], zs.at[k], zr.at[k], to)
        for k, to in enumerate(zpeers)
    ]
    xall = [xpeer[d] for d in (2, 1, -1)]
    yall = [ypeer[d] for d in (2, 1, -1)]
    dxs = [
        send(dbuf.at[y, x, here], dbuf.at[y, x, here], ds.at[k], dr.at[k], to)
        for k, to in enumerate(xall)
    ]
    for l in (l_head, l_pin, l_store):
        l.start()
    c_po = send(po, po_v.at[1], csem_s.at[0], csem_r.at[0], peer)
    c_head = send(head, head_v.at[1], csem_s.at[1], csem_r.at[1], peer)

    def split(h):
        p = po_v[h]
        hi = p.astype(BF16).astype(F32)
        rest = p - hi
        mid = rest.astype(BF16).astype(F32)
        low = rest - mid
        w_v[h] = jnp.concatenate([hi, mid, low, jnp.zeros_like(p)], axis=0).astype(BF16)

    lane = lax.broadcasted_iota(jnp.int32, (1, 128), 1)
    first = lane < 64

    nq = 256
    row = lax.broadcasted_iota(jnp.int32, (nq, 1), 0)
    ry, rx, rzl, rzh, ri = (
        row // 64, (row // 16) % 4, (row // 8) % 2, (row // 2) % 4, row % 2,
    )
    query = 2 * (((rzl * 4 + rx) * 2 + c) * 16 + rzh * 4 + ry) + ri
    ids = lax.broadcasted_iota(jnp.int32, (1, 512), 1)
    l_tgt.wait()
    wanted = jnp.sum(
        jnp.where(ids == query, tgt_v[...].astype(F32), 0.0), axis=1, keepdims=True
    )

    def sum_terms(a, b):
        half = a + pltpu.roll(a, 64, axis=1)
        return half + (b + pltpu.roll(b, 64, axis=1))

    def target_rows(h):
        base = (((v - c) + lax.rem(c + h, 2)) * 16 + s) * nv
        cols = (lax.broadcasted_iota(jnp.int32, (1, nv), 1) + base).astype(F32)
        hot = jnp.where(cols == wanted, 1.0, 0.0).astype(BF16)
        return lax.dot_general(hot, w_v[h], NT, preferred_element_type=F32)

    l_po.wait()
    split(0)
    t0 = target_rows(0)
    c_po.wait_recv()
    split(1)
    t01 = t0 + target_rows(1)
    t = sum_terms(t01[:, :128], t01[:, 128:]).reshape(4, 64, 128)
    t = jnp.where(first, t[:2], t[2:]).reshape(2, 4, 2, 8, 128)
    for k in range(2):
        pm[:, :, 4 + k] = t[k]
    for copy in dxs:
        copy.wait_recv()
    dcolumn = dbuf.at[y, :, here]
    dys = [send(dcolumn, dcolumn, ds.at[3 + k], dr.at[3 + k], to) for k, to in enumerate(yall)]
    for k in zcopies:
        k.wait_recv()
    rows8 = lax.broadcasted_iota(jnp.int32, (8, 1), 0)

    def sixteen(piece):
        halves = []
        for tile in range(2):
            made = None
            for p in range(4):
                pair = piece(tile * 4 + p).astype(F32)
                for i in range(2):
                    row_ = jnp.broadcast_to(pair[i : i + 1], (8, pair.shape[1]))
                    made = row_ if made is None else jnp.where(rows8 == 2 * p + i, row_, made)
            halves.append(made)
        return jnp.concatenate(halves, axis=0).astype(BF16)

    quarter = (half // 256) * 128

    class Order:
        def __init__(self, base, sem, apeer, bpeer, block):
            self.cols = pl.ds(base, half)
            self.part = {1: pl.ds(base, quarter), -1: pl.ds(base + quarter, half - quarter)}
            self.sem, self.apeer, self.bpeer, self.block = sem, apeer, bpeer, block
            self.near, self.bnear, self.bfar = {}, {}, {}

        def put(self, j, block, cols, to):
            view = hbuf.at[block[0], block[1], :, cols]
            return send(view, view, gs.at[self.sem + j], gr.at[self.sem + j], to)

        def own(self):
            for k, d in enumerate((1, -1, 2)):
                self.near[d] = self.put(k, self.block(0, 0), self.cols, self.apeer[d])

        def onward(self, j, da):
            for k, d in enumerate((1, -1)):
                self.bnear[da, d] = self.put(4 + j * 2 + k, self.block(da, 0), self.cols, self.bpeer[d])
            if j in (2, 3,):
                self.bfar[da, 2] = self.put(12 + j * 2, self.block(da, 0), self.cols, self.bpeer[2])

        def bpass_on(self, j, da):
            for k, d in enumerate((1, -1)):
                self.bnear[da, d].wait_recv()
                if j in (2, 3,):
                    continue
                self.bfar[da, d] = self.put(12 + j * 2 + k, self.block(da, -d), self.part[d], self.bpeer[d])

    orders = [
        Order(0, 0, xpeer, ypeer, lambda a, b: (plus(y, b, 4), plus(x, a, 4))),
        Order(half, 20, ypeer, xpeer, lambda a, b: (plus(y, a, 4), plus(x, b, 4))),
    ]
    for o, base in zip(orders, (0, half)):
        for n in range(base, base + half, half // 2 // 128 * 128):
            span = pl.ds(n, min(half // 2 // 128 * 128, base + half - n))
            hbuf[y, x, :, span] = sixteen(lambda p: zbuf[p, :, span])
        o.own()
    for o in orders:
        o.onward(0, 0)
    for copy in dys:
        copy.wait_recv()
    dplane = dbuf.at[:, :, here]
    dzs = [
        send(dplane, dplane, ds.at[6 + k], dr.at[6 + k], to) for k, to in enumerate(zpeers)
    ]
    for k, d in enumerate((1, -1)):
        for o in orders:
            o.near[d].wait_recv()
            o.onward(1 + k, -d)

    for o in orders:
        o.near[2].wait_recv()
        o.onward(3, 2)
    for o in orders:
        o.bpass_on(0, 0)
    for k, d in enumerate((1, -1)):
        for o in orders:
            o.bpass_on(1 + k, -d)

    l_head.wait()
    c_head.wait_recv()

    for o in orders:
        o.bpass_on(3, 2)
    for copy in dzs:
        copy.wait_recv()

    def last_columns(k, carry):
        b, a = lax.div(k, 4), lax.rem(k, 4)
        hbuf[b, a, :, dcols] = sixteen(lambda p: dbuf[b, a, p])
        return carry

    lax.fori_loop(0, 16, last_columns, 0)
    for o in orders:
        for copy in o.bfar.values():
            copy.wait_recv()
    tcopies = [
        send(pm.at[a, b, pl.ds(4, 2)], rb1.at[k, pl.ds(4, 2)], ts.at[k], tr.at[k], r1dev[k])
        for k, (a, b) in enumerate(r1)
    ]
    left = hbuf[...].reshape(nq, width)
    for h in range(2):
        part = lax.dot_general(left, head_v[h], NT, preferred_element_type=F32)
        acc[h] = part.reshape(4, 4, 16, nv)

    step = 512
    flat = [acc[h].reshape(nq, nv) for h in range(2)]
    peak = jnp.maximum(
        jnp.max(flat[0], axis=1, keepdims=True), jnp.max(flat[1], axis=1, keepdims=True)
    )
    sides = []
    denom = jnp.zeros((nq, 1), F32)
    for h in range(2):
        e = jnp.exp(flat[h] - peak)
        denom = denom + jnp.sum(e, axis=1, keepdims=True)
        hi = e.astype(BF16)
        low = (e - hi.astype(F32)).astype(BF16)
        sides.append(
            lax.dot_general(hi, w_v[h], NT, preferred_element_type=F32)
            + lax.dot_general(low, w_v[h], NT, preferred_element_type=F32)
        )
    both = sides[0] + sides[1]
    both = sum_terms(both[:, :128], both[:, 128:])
    is_peak = (lane >= 64) & (lane < 96)
    packed = jnp.where(first, both, jnp.where(is_peak, peak, denom))
    packed = packed.reshape(4, 4, 2, 8, 128)
    for k in range(4):
        pm[:, :, k] = packed[k]
    rcopies = [
        send(
            pm.at[a, b, pl.ds(0, 4)], rb1.at[k, pl.ds(0, 4)], rs.at[k], rr.at[k], r1dev[k]
        )
        for k, (a, b) in enumerate(r1)
    ]

    l_pin.wait()

    def widths(i, carry):
        span = pl.ds(pl.multiple_of(i * step, step), step)
        left = hbuf[:, x, :, span].reshape(64, step)
        return carry + lax.dot_general(left, pin_v[:, span], NT, preferred_element_type=F32)

    w = lax.fori_loop(0, width // step, widths, jnp.zeros((64, 64), F32))
    wd[...] = jnp.concatenate([w, w], axis=1).reshape(4, 2, 8, 128)
    width2 = wd[:, zl].reshape(32, 128)

    def combine(parts):
        most = parts[0]
        for p in parts[1:]:
            most = jnp.maximum(most, p)
        m = most[:, 64:65]
        sums = None
        for p in parts:
            term = p * jnp.exp(p[:, 64:65] - m)
            sums = term if sums is None else sums + term
        return jnp.where(is_peak, most, sums)

    def waited(copies, buf):
        got = []
        for k, copy in enumerate(copies):
            copy.wait_recv()
            got.append(buf[k, :4].reshape(32, 128))
        return got

    def target_sum(total, copies, buf):
        for k, copy in enumerate(copies):
            copy.wait_recv()
            total = total + buf[k, 4:].reshape(16, 128)
        return total

    sums_of, rows_of = pl.ds(0, 4), pl.ds(4, 2)

    def step_on(held, bufs, first_sem, sems, part, to_all):
        return [
            send(held.at[part], bufs.at[k, part], sems[0].at[first_sem + k], sems[1].at[first_sem + k], to)
            for k, to in enumerate(to_all)
        ]

    rows = target_sum(pm[x, zl, 4:].reshape(16, 128), tcopies, rb1)
    rs2[4:] = rows.reshape(2, 8, 128)
    tcopies = step_on(rs2, rb2, 7, (ts, tr), rows_of, r2dev)
    mine = pm[x, zl, :4].reshape(32, 128)
    mine = combine([mine] + waited(rcopies, rb1))
    rs2[:4] = mine.reshape(4, 8, 128)
    rcopies = step_on(rs2, rb2, 7, (rs, rr), sums_of, r2dev)
    rows = target_sum(rows, tcopies, rb2)
    rs3[4:] = rows.reshape(2, 8, 128)
    tcopies = step_on(rs3, rb3, 10, (ts, tr), rows_of, r3dev)
    mine = combine([mine] + waited(rcopies, rb2))
    rs3[:4] = mine.reshape(4, 8, 128)
    rcopies = step_on(rs3, rb3, 10, (rs, rr), sums_of, r3dev)
    rows = target_sum(rows, tcopies, rb3)
    mine = combine([mine] + waited(rcopies, rb3))

    side = mine / mine[:, 96:97] - jnp.concatenate([rows, pltpu.roll(rows, 64, axis=1)], axis=0)
    for b in range(32):
        pair = jnp.where(first, side[:, 2 * b : 2 * b + 1], side[:, 2 * b + 1 : 2 * b + 2])
        kron[:, b * 128 : (b + 1) * 128] = (pair * width2).astype(BF16)
    l_store.wait()
    scores = lax.dot_general(kron[...], store_v[...], NT, preferred_element_type=F32)
    pairs = lax.broadcasted_iota(jnp.int32, (8, 1), 0) // 2
    for a in range(4):
        made = None
        for b in range(4):
            turned = scores[b * 8 : b * 8 + 8]
            if a != b:
                turned = pltpu.roll(turned, (2 * b - 2 * a) % 8, axis=0)
            made = turned if made is None else jnp.where(pairs == b, turned, made)
        out[a * 8 : a * 8 + 8] = made

    for copy in started:
        copy.wait_send()


def local(hidden_states, head, proj_out, proj_in, store, targets):
    nv, width = head.shape
    vm = pltpu.VMEM
    dma = pltpu.SemaphoreType.DMA
    return pl.pallas_call(
        kernel,
        out_shape=jax.ShapeDtypeStruct((32, 128), F32),
        in_specs=[pl.BlockSpec(memory_space=pltpu.HBM)] * 6,
        out_specs=pl.BlockSpec(memory_space=pltpu.VMEM),
        scratch_shapes=[
            vm((1, 512), jnp.int32),
            vm((8, 2, width), BF16),
            vm((4, 4, 16, width), BF16),
            vm((2, nv, width), BF16),
            vm((2, 64, nv), F32),
            vm((2, 256, nv), BF16),
            vm((64, width), BF16),
            vm((128, width), BF16),
            vm((2, 4, 4, 16, nv), F32),
            vm((4, 2, 6, 8, 128), F32),
            vm((7, 6, 8, 128), F32),
            vm((3, 6, 8, 128), F32),
            vm((3, 6, 8, 128), F32),
            vm((6, 8, 128), F32),
            vm((6, 8, 128), F32),
            vm((4, 2, 8, 128), F32),
            vm((32, width), BF16),
            dma((7,)), dma((2,)), dma((2,)), dma((7,)), dma((7,)),
            dma((40,)), dma((40,)), dma((13,)), dma((13,)), dma((13,)), dma((13,)),
            vm((4, 4, 8, 2, ZSHARE), BF16), dma((13,)), dma((13,)),
        ],
        compiler_params=pltpu.CompilerParams(
            collective_id=0, has_side_effects=True, vmem_limit_bytes=64 * 2**20 - 2**16
        ),
        cost_estimate=pl.CostEstimate(flops=2 * 10**9, bytes_accessed=10**7, transcendentals=0),
    )(hidden_states, head, proj_out.T, proj_in.T, store, targets.reshape(1, -1))

def solution(mesh):
    placed = (
        P(("vocab", "store"), None),
        P(("vocab", "store"), None),
        P(("vocab", "store"), None),
        P(),
        P("store", None),
        P(),
    )
    return jax.shard_map(
        local, mesh=mesh, in_specs=placed, out_specs=P("vocab", "store"), check_vma=False
    )
```
